32 devices in a mesh: seq: 8 (over z, x), batch: 4 (over y, core).
Axes of the slice: x: 2, y: 2, z: 4, core: 2. Of those that a mesh axis runs over, the one named last changes fastest.
Arguments:
- hidden_in: bfloat16 [16, 1024, 768], P('batch', 'seq'), may hold values from -6 to 6
- lengths: int32 [16], P('batch'), may hold values from 128 to 1024, as said below
- selected: int32 [16, 16, 12, 64], P('batch', 'seq'), may hold values from 0 to 15
- in_proj: bfloat16 [768, 2304], replicated, may hold values from -0.21875 to 0.21875
- scorer: bfloat16 [768, 12], replicated, may hold values from -0.21875 to 0.21875
- out_proj: bfloat16 [768, 768], replicated, may hold values from -0.625 to 0.625
- up_proj: bfloat16 [768, 3072], replicated, may hold values from -0.21875 to 0.21875
- up_bias: bfloat16 [3072], replicated, may hold values from -3 to 3
- down_proj: bfloat16 [3072, 768], replicated, may hold values from -0.109375 to 0.109375
- first_gain: bfloat16 [768], replicated, may hold values from 0.25 to 1.75
- first_shift: bfloat16 [768], replicated, may hold values from -2 to 2
- second_gain: bfloat16 [768], replicated, may hold values from 0.25 to 1.75
- second_shift: bfloat16 [768], replicated, may hold values from -2 to 2
- cotangent: bfloat16 [16, 1024, 768], P('batch', 'seq'), may hold values from -6 to 6
Outputs:
- block_out: bfloat16 [16, 1024, 768], P('batch', 'seq')
- grad_input: bfloat16 [16, 1024, 768], P('batch', 'seq')
- grad_in_proj: float32 [768, 2304], P('seq')
- grad_scorer: float32 [768, 12], P('seq')
- grad_out_proj: float32 [768, 768], P('seq')
- grad_up_proj: float32 [768, 3072], P('seq')
- grad_up_bias: float32 [3072], P('seq')
- grad_down_proj: float32 [3072, 768], P('seq')
- grad_first_gain: float32 [768], P('seq')
- grad_first_shift: float32 [768], P('seq')
- grad_second_gain: float32 [768], P('seq')
- grad_second_shift: float32 [768], P('seq')
The draws below stay inside these ranges and needn't reach their ends.
Inputs may be any that keep to these rules, and one draw needn't show every extreme that they name: `lengths`: in every group of 4 sequences on one index of batch, one sequence, drawn from the seed, has length 1024.
All inputs are finite; a program needn't handle non-finite values.
Results may differ from the reference program's by a relative error of at most 0.015.
Values may be sent and summed in bfloat16 or wider, within the bound.
A program may use at most 192 MiB of HBM per device.

```python
import math
import jax
import jax.numpy as jnp
from jax import lax

D = 768
HEADS = 12
FF = 3072
TILE = 64
WIN = 64
SEL = 64
TOK_DEV = 128
SEQS = 4
LEN = 1024
NT = 16
NSEQS = 16


def draw_lengths(key, part):
    key = jax.random.fold_in(key, 11)
    key_lengths, key_choice = jax.random.split(key)
    groups = NSEQS // SEQS
    drawn_lengths = jax.random.randint(key_lengths, (groups, SEQS), TOK_DEV, LEN + 1)
    chosen_slot = jax.random.randint(key_choice, (groups, 1), 0, SEQS)
    slot_index = jnp.arange(SEQS, dtype=jnp.int32)[None, :]
    return jnp.where(slot_index == chosen_slot, LEN, drawn_lengths).reshape(NSEQS).astype(jnp.int32)


def set_ends(values, key, least, high):
    place = [jax.random.randint(jax.random.fold_in(key, axis), (), 0, length) for axis, length in enumerate(values.shape)]
    widest = values.shape.index(max(values.shape))
    next_to = place[:widest] + [(place[widest] + 1) % values.shape[widest]] + place[widest + 1:]
    return values.at[tuple(place)].set(least).at[tuple(next_to)].set(high)


def levels(stream_key, dims, shards, smallest, top_value):
    def one(dim, blocks):
        heights = jax.random.uniform(jax.random.fold_in(jax.random.fold_in(stream_key, 6), dim), (blocks,), jnp.float32, smallest / len(shards), top_value / len(shards))
        return jnp.repeat(jnp.exp(heights), dims[dim] // blocks).reshape((-1,) + (1,) * (len(dims) - dim - 1))

    level = one(*shards[0])
    for cut in shards[1:]:
        level = level * one(*cut)
    return level


def bell_draw(key, extent, deviation, reach, pieces=(), held_as=jnp.bfloat16):
    drawn = deviation * jax.random.normal(key, extent, jnp.float32)
    if pieces:
        drawn = drawn * levels(key, extent, pieces, -0.22, 0.18)
    return jnp.clip(drawn, -reach, reach).astype(held_as)


def setup_inputs(seed: int = 0) -> dict:
    seeds = jax.random.split(jax.random.key(seed), 15)
    hidden_in = bell_draw(seeds[0], (NSEQS, LEN, D), 1.0, 6.0, ((0, 4), (1, 8)))
    lengths = draw_lengths(jax.random.fold_in(seeds[14], 71), 0)
    selected = set_ends(jax.random.randint(seeds[2], (NSEQS, NT, HEADS, SEL), 0, NT), jax.random.fold_in(seeds[2], 1), 0, NT - 1).astype(jnp.int32)
    in_proj = bell_draw(seeds[3], (D, 3 * D), D ** -0.5, 0.21875)
    scorer = bell_draw(seeds[4], (D, HEADS), D ** -0.5, 0.21875)
    out_proj = bell_draw(seeds[5], (D, D), (D // 8) ** -0.5, 0.625)
    up_proj = bell_draw(seeds[6], (D, FF), D ** -0.5, 0.21875)
    up_bias = bell_draw(seeds[7], (FF,), 0.5, 3.0)
    down_proj = bell_draw(seeds[8], (FF, D), FF ** -0.5, 0.109375)
    first_gain = jnp.clip(1.0 + 0.15 * jax.random.normal(seeds[9], (D,), jnp.float32), 0.25, 1.75).astype(jnp.bfloat16)
    first_shift = bell_draw(seeds[10], (D,), 0.3, 2.0)
    second_gain = jnp.clip(1.0 + 0.15 * jax.random.normal(seeds[11], (D,), jnp.float32), 0.25, 1.75).astype(jnp.bfloat16)
    second_shift = bell_draw(seeds[12], (D,), 0.3, 2.0)
    cotangent = bell_draw(seeds[13], (NSEQS, LEN, D), 1.0, 6.0, ((0, 4), (1, 8)))
    return dict(hidden_in=hidden_in, lengths=lengths, selected=selected, in_proj=in_proj, scorer=scorer, out_proj=out_proj, up_proj=up_proj, up_bias=up_bias, down_proj=down_proj, first_gain=first_gain, first_shift=first_shift, second_gain=second_gain, second_shift=second_shift, cotangent=cotangent)


@jax.custom_vjp
def low(v):
    return lax.optimization_barrier(v.astype(jnp.bfloat16)).astype(jnp.float32)

@jax.custom_vjp
def low_back(v):
    return v

def low_keep(v):
    return (low(v), None)

def low_pass(kept, grad):
    return (grad,)

def back_keep(v):
    return (v, None)

def back_low(kept, grad):
    return (low(grad),)
low.defvjp(low_keep, low_pass)
low_back.defvjp(back_keep, back_low)
EPS = 1e-05
NEG = -1e+30
HIGHEST = lax.Precision.HIGHEST

def layer_norm(values, gain, shift):
    average = lax.optimization_barrier(jnp.mean(values, axis=-1, keepdims=True))
    centered = values - average
    variance = lax.optimization_barrier(jnp.mean(centered * centered, axis=-1, keepdims=True))
    return centered * lax.rsqrt(variance + EPS) * gain + shift

def window_mask(tile_ids):
    row_index = lax.broadcasted_iota(jnp.int32, (TILE, 2 * TILE), 0)
    col_index = lax.broadcasted_iota(jnp.int32, (TILE, 2 * TILE), 1)
    distance = TILE + row_index - col_index
    inside = (distance >= 0) & (distance <= WIN)
    exists = (tile_ids > 0)[:, None, None] | (col_index >= TILE)[None]
    return inside[None] & exists

def allowed_mask(tile_ids, picks):
    lead = picks.shape[:3]
    near_mask = jnp.broadcast_to(window_mask(tile_ids)[None, :, None], lead + (TILE, 2 * TILE))
    far_mask = picks[:, :, :, None, :] < tile_ids[None, :, None, None, None]
    far_mask = jnp.broadcast_to(far_mask, lead + (TILE, picks.shape[3]))
    return jnp.concatenate([near_mask, far_mask], -1)

def one_sequence(params, hidden, length, picks):
    in_proj, scorer, out_proj, up_proj, up_bias, down_proj, first_gain, first_shift, second_gain, second_shift = params
    model_width = hidden.shape[1]
    head_count = scorer.shape[1]
    head_size = model_width // head_count
    tile_count = hidden.shape[0] // TILE
    normed = low(layer_norm(hidden, first_gain, first_shift))
    packed = low(low_back(jnp.dot(normed, in_proj, precision=HIGHEST)))
    weights = jax.nn.sigmoid(low_back(jnp.dot(normed, scorer, precision=HIGHEST)))
    shaped = packed.reshape(1, tile_count, TILE, 3, head_count, head_size)
    query_tiles = shaped[:, :, :, 0]
    pair_tiles = shaped[:, :, :, 1:]
    tile_weights = weights.reshape(1, tile_count, TILE, head_count, 1)
    root_tile = math.sqrt(TILE)
    key_comp = low(lax.optimization_barrier(jnp.sum(tile_weights * pair_tiles[:, :, :, 0], axis=2)) / root_tile)
    value_comp = low(lax.optimization_barrier(jnp.sum(tile_weights * pair_tiles[:, :, :, 1], axis=2)) / root_tile)
    head_ids = jnp.arange(head_count, dtype=jnp.int32)[None, :, None]
    key_pick = key_comp[0][picks, head_ids][None]
    value_pick = value_comp[0][picks, head_ids][None]
    before = jnp.concatenate([jnp.zeros_like(pair_tiles[:, :1]), pair_tiles[:, :-1]], 1)
    window_pairs = jnp.concatenate([before, pair_tiles], 2)
    key_window = window_pairs[:, :, :, 0]
    value_window = window_pairs[:, :, :, 1]
    tile_ids = jnp.arange(tile_count, dtype=jnp.int32)
    allowed = allowed_mask(tile_ids, picks[None])
    score_scale = 1.0 / math.sqrt(head_size)
    near = jnp.einsum('spahd,spbhd->sphab', query_tiles, key_window, precision=HIGHEST)
    far = jnp.einsum('spahd,sphjd->sphaj', query_tiles, key_pick, precision=HIGHEST)
    scores = low_back(jnp.concatenate([near, far], -1) * score_scale)
    probs = low(jax.nn.softmax(jnp.where(allowed, scores, NEG), axis=-1))
    span = 2 * TILE
    near_out = jnp.einsum('sphab,spbhd->spahd', probs[..., :span], value_window, precision=HIGHEST)
    far_out = jnp.einsum('sphaj,sphjd->spahd', probs[..., span:], value_pick, precision=HIGHEST)
    attended = low(low_back((near_out + far_out).reshape(hidden.shape[0], model_width)))
    projected = low_back(jnp.dot(attended, out_proj, precision=HIGHEST))
    middle = hidden + projected
    normed_two = low(layer_norm(middle, second_gain, second_shift))
    upper = low_back(jnp.dot(normed_two, up_proj, precision=HIGHEST) + up_bias)
    active = low(jax.nn.gelu(upper, approximate=True))
    lowered = low_back(jnp.dot(active, down_proj, precision=HIGHEST))
    result = middle + lowered
    valid = (jnp.arange(hidden.shape[0], dtype=jnp.int32) < length)[:, None]
    return jnp.where(valid, result, 0.0)

def reference(hidden_in, lengths, selected, in_proj, scorer, out_proj, up_proj, up_bias, down_proj, first_gain, first_shift, second_gain, second_shift, cotangent):
    params = (in_proj.astype(jnp.float32), scorer.astype(jnp.float32), out_proj.astype(jnp.float32), up_proj.astype(jnp.float32), up_bias.astype(jnp.float32), down_proj.astype(jnp.float32), first_gain.astype(jnp.float32), first_shift.astype(jnp.float32), second_gain.astype(jnp.float32), second_shift.astype(jnp.float32))

    def forward(inputs, weights_all):

        def per_sequence(hidden, length, picks):
            return one_sequence(weights_all, hidden, length, picks)
        saved_fn = jax.checkpoint(per_sequence)

        def apply_one(sequence_item):
            return saved_fn(sequence_item[0], sequence_item[1], sequence_item[2])
        return lax.map(apply_one, (inputs, lengths, selected))
    result, pull = jax.vjp(forward, hidden_in.astype(jnp.float32), params)
    grad_hidden, grads = pull(cotangent.astype(jnp.float32))
    return (result.astype(jnp.bfloat16), grad_hidden.astype(jnp.bfloat16), grads[0], grads[1], grads[2], grads[3], grads[4], grads[5], grads[6], grads[7], grads[8], grads[9])
```

```python
from functools import partial
import math

import jax
import jax.numpy as jnp
from jax import lax
from jax.experimental import pallas as pl
from jax.experimental.pallas import tpu as pltpu
from jax.sharding import PartitionSpec as P

TILE = 64
WIN = 64


EPS = 1e-05
NEG = -1e30


def passed_along(block, axis, distance):
    devices = range(lax.axis_size(axis))
    route = [(i - distance, i) for i in devices if i - distance in devices]
    return lax.ppermute(block, axis, route)


def cut_along(value, dim, length):
    before, after = (value.shape[:dim], value.shape[dim + 1 :])
    return jnp.moveaxis(value.reshape(*before, length, -1, *after), dim, 0)


def sum_at_owner(value, axis, dim):
    parts = cut_along(value, dim, lax.axis_size(axis))
    arrived = lax.all_to_all(parts, axis, split_axis=0, concat_axis=0, tiled=True)
    return arrived.astype(jnp.float32).sum(axis=0)


def layer_norm(values, gain, shift):
    average = jnp.mean(values, axis=-1, keepdims=True)
    centered = values - average
    variance = jnp.mean(centered * centered, axis=-1, keepdims=True)
    return centered * lax.rsqrt(variance + EPS) * gain + shift


def window_mask(tile_ids):
    row_index = lax.broadcasted_iota(jnp.int32, (TILE, 2 * TILE), 0)
    col_index = lax.broadcasted_iota(jnp.int32, (TILE, 2 * TILE), 1)
    distance = TILE + row_index - col_index
    inside = (distance >= 0) & (distance <= WIN)
    exists = (tile_ids > 0)[:, None, None] | (col_index >= TILE)[None]
    return inside[None] & exists


def allowed_mask(tile_ids, picks):
    lead = picks.shape[:3]
    near_mask = jnp.broadcast_to(window_mask(tile_ids)[None, :, None], lead + (TILE, 2 * TILE))
    far_mask = picks[:, :, :, None, :] < tile_ids[None, :, None, None, None]
    far_mask = jnp.broadcast_to(far_mask, lead + (TILE, picks.shape[3]))
    return jnp.concatenate([near_mask, far_mask], -1)


def attention_scores(query_tiles, key_window, key_pick, allowed, score_scale):
    near = jnp.einsum(
        "spahd,spbhd->sphab", query_tiles, key_window, preferred_element_type=jnp.float32
    )
    far = jnp.einsum(
        "spahd,sphjd->sphaj", query_tiles, key_pick, preferred_element_type=jnp.float32
    )
    return jnp.where(allowed, jnp.concatenate([near, far], -1) * score_scale, NEG)


MESH_ID = pl.DeviceIdType.MESH


class Place:
    def __init__(self, seq_bits):
        self.seq = lax.axis_index("seq")
        self.batch = lax.axis_index("batch")
        self.bits = {"k": self.batch % 2, "y": self.batch // 2}
        for i in range(seq_bits):
            self.bits["b%d" % i] = (self.seq // 2**i) % 2

    def partner(self, dim):
        flip = 1 - 2 * self.bits[dim]
        if dim == "k":
            return (self.seq, self.batch + flip)
        if dim == "y":
            return (self.seq, self.batch + 2 * flip)
        return (self.seq + flip * 2 ** int(dim[1:]), self.batch)


def pick(axes, fixed):
    return tuple(fixed[a] if a in fixed else slice(None) for a in axes)


class Flow:
    def __init__(self, place, axes, order, rows, cols, item, bufs, fin, send, recv):
        self.place, self.axes = place, axes
        self.dims = ("k",) + order
        self.rows, self.cols = rows, cols
        self.item, self.bufs, self.fin = item, bufs, fin
        self.send, self.recv = send, recv
        self.copies = []

    def fixed(self, count):
        return {d: self.place.bits[d] for d in self.dims[:count]}

    def copy(self, src, dst, dim):
        j = len(self.copies)
        cp = pltpu.make_async_remote_copy(
            src_ref=src,
            dst_ref=dst,
            send_sem=self.send.at[j],
            recv_sem=self.recv.at[j],
            device_id=self.place.partner(dim),
            device_id_type=MESH_ID,
        )
        cp.start()
        self.copies.append(cp)

    def add(self, j):
        fixed = self.fixed(j + 1)
        free = [a for a in self.axes if a not in fixed]
        count = 2 ** len(free)
        last = not free

        def body(i, carry):
            at = {a: (i // 2**n) % 2 for n, a in enumerate(free)}
            here = self.item.at[pick(self.axes, {**fixed, **at})]
            there = self.bufs[j].at[pick(free, at)]
            total = here[...] + there[...]
            if last:
                self.fin[self.place.bits["k"], self.place.bits["y"]] = total
            else:
                here[...] = total
            return carry

        if last:
            body(0, 0)
        else:
            lax.fori_loop(0, count, body, 0)

    def advance(self):
        j = len(self.copies)
        bits = self.place.bits
        if j:
            self.copies[-1].wait_recv()
            if j <= 5:
                self.add(j - 1)
        if j < 5:
            dim = self.dims[j]
            other = {**self.fixed(j), dim: 1 - bits[dim]}
            self.copy(self.item.at[pick(self.axes, other)], self.bufs[j], dim)
        elif j == 5:
            piece = self.fin.at[bits["k"], bits["y"]]
            self.copy(piece, piece, "y")
        elif j == 6:
            self.copy(self.fin.at[bits["k"]], self.fin.at[bits["k"]], "k")
        else:
            return True
        return False

    def finish(self):
        for cp in self.copies:
            cp.wait_send()


def greet(place, dims):
    barrier = pltpu.get_barrier_semaphore()
    for dim in dims:
        pl.semaphore_signal(barrier, inc=1, device_id=place.partner(dim), device_id_type=MESH_ID)
    pl.semaphore_wait(barrier, len(dims))


def recv_shapes(rows, cols):
    return [pltpu.VMEM((2,) * (4 - j) + (rows, cols), jnp.bfloat16) for j in range(5)]


KCOL = ("k", "b2", "b1", "b0", "y")
KROW = ("b2", "b1", "b0", "k", "y")
ORDERS = {"A": ("b0", "y", "b1", "b2"), "B": ("y", "b0", "b1", "b2"), "C": ("b1", "b2", "b0", "y")}


def reduce_kernel(plan, *refs):
    count = len(plan)
    ins, outs, refs = refs[:count], refs[count : 2 * count], refs[2 * count :]
    items, refs = refs[:count], refs[count:]
    bufs, refs = refs[: 5 * count], refs[5 * count :]
    fins, refs = refs[:count], refs[count:]
    send, recv, local = refs
    place = Place(3)
    loads = []
    for i in range(count):
        cp = pltpu.make_async_copy(ins[i], items[i], local.at[i])
        cp.start()
        loads.append(cp)
    greet(place, ("k", "y", "b0", "b1", "b2"))
    flows = []
    for i, (axes, order, rows, cols) in enumerate(plan):
        flows.append(Flow(place, axes, ORDERS[order], rows, cols, items[i], bufs[5 * i : 5 * i + 5], fins[i], send.at[i], recv.at[i]))
    for i in range(count):
        loads[i].wait()
        flows[i].advance()
    stores = []
    for step in range(7):
        for i in range(count):
            if flows[i].advance():
                cp = pltpu.make_async_copy(fins[i], outs[i], local.at[i])
                cp.start()
                stores.append(cp)
    for flow in flows:
        flow.finish()
    for cp in stores:
        cp.wait()


def reduce_items(items, plan):
    count = len(plan)
    scratch = [pltpu.VMEM(item.shape, jnp.bfloat16) for item in items]
    for axes, order, rows, cols in plan:
        scratch += recv_shapes(rows, cols)
    scratch += [pltpu.VMEM((2, 2, rows, cols), jnp.bfloat16) for axes, order, rows, cols in plan]
    scratch += [pltpu.SemaphoreType.DMA((count, 7)), pltpu.SemaphoreType.DMA((count, 7)), pltpu.SemaphoreType.DMA((count,))]
    return pl.pallas_call(
        partial(reduce_kernel, plan),
        out_shape=[jax.ShapeDtypeStruct((2, 2, rows, cols), jnp.bfloat16) for axes, order, rows, cols in plan],
        in_specs=[pl.BlockSpec(memory_space=pl.ANY)] * count,
        out_specs=[pl.BlockSpec(memory_space=pl.ANY)] * count,
        scratch_shapes=scratch,
        compiler_params=pltpu.CompilerParams(collective_id=0, has_side_effects=True, vmem_limit_bytes=56 * 2**20),
        name="reduce",
    )(*items)


def by_columns(grad, width):
    low = grad.astype(jnp.bfloat16).reshape(2, 2, 2, 2, 48, width // 256, 2, 128)
    return jnp.transpose(low, (6, 0, 1, 2, 3, 4, 5, 7)).reshape(2, 2, 2, 2, 2, 48, width // 2)


def from_columns(fin):
    width = fin.shape[-1]
    parts = fin.reshape(2, 2, 48, width // 128, 128)
    return jnp.transpose(parts, (1, 2, 3, 0, 4)).reshape(96, 2 * width).astype(jnp.float32)


def reduce_all(grad_in, grad_score, grad_out, grad_up, grad_up_bias, grad_down, columns):
    plan, items = [], []
    down = grad_down.astype(jnp.bfloat16).reshape(8, 3, 128, 768)
    up = grad_up.reshape(768, 8, 3, 128)
    for c in range(3):
        plan.append((KROW, "ABC"[(2 * c) % 3], 32, 768))
        items.append(down[:, c].reshape(2, 2, 2, 2, 2, 32, 768))
        plan.append((KCOL, "ABC"[(2 * c + 1) % 3], 48, 512))
        items.append(by_columns(up[:, :, c].reshape(768, 1024), 1024))
    plan.append((KCOL, "A", 48, 384))
    items.append(by_columns(grad_out, 768))
    for g in range(3):
        plan.append((KCOL, "BCB"[g], 48, 384))
        items.append(by_columns(grad_in[:, 768 * g : 768 * g + 768], 768))
    bias = jnp.transpose(grad_up_bias.reshape(8, 3, 128), (0, 1, 2))
    right = jnp.zeros((8, 96, 128), jnp.float32).at[:, :3].set(bias).reshape(768, 128)
    left = jnp.concatenate([grad_score] + [c[:, None] for c in columns] + [jnp.zeros((768, 112), jnp.float32)], 1)
    plan.append((KCOL, "A", 48, 128))
    items.append(by_columns(jnp.concatenate([left, right], 1), 256))
    fins = reduce_items(items, plan)
    down_out = jnp.stack([fins[2 * c].reshape(128, 768) for c in range(3)], 0).reshape(384, 768).astype(jnp.float32)
    ups = [from_columns(fins[2 * c + 1]).reshape(96, 8, 1, 128) for c in range(3)]
    up_out = jnp.concatenate(ups, 2).reshape(96, 3072)
    out_out = from_columns(fins[6])
    in_out = jnp.concatenate([from_columns(fins[7 + g]) for g in range(3)], 1)
    misc = from_columns(fins[10])
    return (in_out, misc[:, :12], out_out, up_out, misc[:3, 128:].reshape(384), down_out) + tuple(misc[:, 12 + i] for i in range(4))


def shards(
    hidden_in,
    lengths,
    selected,
    in_proj,
    scorer,
    out_proj,
    up_proj,
    up_bias,
    down_proj,
    first_gain,
    first_shift,
    second_gain,
    second_shift,
    cotangent,
):
    sequences, tokens, model_width = hidden_in.shape
    head_count = scorer.shape[1]
    head_size = model_width // head_count
    tile_count = tokens // TILE
    row_count = sequences * tokens
    span = 2 * TILE
    score_scale = 1.0 / math.sqrt(head_size)
    root_tile = math.sqrt(TILE)
    gain_one = first_gain.astype(jnp.float32)
    shift_one = first_shift.astype(jnp.float32)
    gain_two = second_gain.astype(jnp.float32)
    shift_two = second_shift.astype(jnp.float32)
    hidden = hidden_in.astype(jnp.float32).reshape(row_count, model_width)
    normed = layer_norm(hidden, gain_one, shift_one).astype(jnp.bfloat16)
    packed = jnp.dot(normed, in_proj, preferred_element_type=jnp.float32).astype(jnp.bfloat16)
    weights = jax.nn.sigmoid(jnp.dot(normed, scorer, preferred_element_type=jnp.float32))
    shaped = packed.reshape(sequences, tile_count, TILE, 3, head_count, head_size)
    query_tiles = shaped[:, :, :, 0]
    pair_tiles = shaped[:, :, :, 1:]
    key_float = pair_tiles[:, :, :, 0].astype(jnp.float32)
    value_float = pair_tiles[:, :, :, 1].astype(jnp.float32)
    tile_weights = weights.reshape(sequences, tile_count, TILE, head_count, 1)
    key_comp = jnp.sum(tile_weights * key_float, axis=2) / root_tile
    value_comp = jnp.sum(tile_weights * value_float, axis=2) / root_tile
    compressed = jnp.concatenate(
        [
            key_comp.reshape(sequences, tile_count, model_width),
            value_comp.reshape(sequences, tile_count, model_width),
        ],
        -1,
    ).astype(jnp.bfloat16)
    gathered = lax.all_gather(compressed, "seq", axis=1, tiled=True)
    last_rows = packed.reshape(sequences, tokens, 3 * model_width)[:, tokens - TILE :, model_width:]
    previous = passed_along(last_rows, "seq", 1)
    previous = previous.reshape(sequences, 1, TILE, 2, head_count, head_size)
    before = jnp.concatenate([previous, pair_tiles[:, :-1]], 1)
    window_pairs = jnp.concatenate([before, pair_tiles], 2)
    key_window = window_pairs[:, :, :, 0]
    value_window = window_pairs[:, :, :, 1]
    tile_total = gathered.shape[1]
    choose = (selected[..., None] == jnp.arange(tile_total, dtype=jnp.int32)).astype(jnp.bfloat16)
    gathered_split = gathered.reshape(sequences, tile_total, 2, head_count, head_size)
    key_pick = jnp.einsum(
        "sphjn,snhd->sphjd", choose, gathered_split[:, :, 0], preferred_element_type=jnp.float32
    ).astype(jnp.bfloat16)
    value_pick = jnp.einsum(
        "sphjn,snhd->sphjd", choose, gathered_split[:, :, 1], preferred_element_type=jnp.float32
    ).astype(jnp.bfloat16)
    tile_ids = lax.axis_index("seq") * tile_count + jnp.arange(tile_count, dtype=jnp.int32)
    allowed = allowed_mask(tile_ids, selected)
    scores = attention_scores(query_tiles, key_window, key_pick, allowed, score_scale)
    top_score = jnp.max(scores, -1, keepdims=True)
    log_total = top_score + jnp.log(jnp.sum(jnp.exp(scores - top_score), -1, keepdims=True))
    probs_low = jnp.exp(scores - log_total).astype(jnp.bfloat16)
    near_out = jnp.einsum(
        "sphab,spbhd->spahd",
        probs_low[..., :span],
        value_window,
        preferred_element_type=jnp.float32,
    )
    far_out = jnp.einsum(
        "sphaj,sphjd->spahd", probs_low[..., span:], value_pick, preferred_element_type=jnp.float32
    )
    attended = (near_out + far_out).reshape(row_count, model_width).astype(jnp.bfloat16)
    middle = hidden + jnp.dot(attended, out_proj, preferred_element_type=jnp.float32)
    normed_two = layer_norm(middle, gain_two, shift_two).astype(jnp.bfloat16)
    upper = jnp.dot(normed_two, up_proj, preferred_element_type=jnp.float32) + up_bias.astype(
        jnp.float32
    )
    gelu_fn = partial(jax.nn.gelu, approximate=True)
    active, gelu_pull = jax.vjp(gelu_fn, upper)
    active = active.astype(jnp.bfloat16)
    result = middle + jnp.dot(active, down_proj, preferred_element_type=jnp.float32)
    positions = lax.axis_index("seq") * tokens + jnp.arange(tokens, dtype=jnp.int32)
    valid = (positions[None, :] < lengths[:, None]).reshape(row_count, 1)
    block_out = (
        jnp.where(valid, result, 0.0).astype(jnp.bfloat16).reshape(sequences, tokens, model_width)
    )
    d_result = jnp.where(valid, cotangent.astype(jnp.float32).reshape(row_count, model_width), 0.0)
    d_result_low = d_result.astype(jnp.bfloat16)
    grad_down = jnp.einsum("rf,rd->fd", active, d_result_low, preferred_element_type=jnp.float32)
    d_active = jnp.einsum("rd,fd->rf", d_result_low, down_proj, preferred_element_type=jnp.float32)
    d_upper = gelu_pull(d_active)[0].astype(jnp.bfloat16)
    grad_up = jnp.einsum("rd,rf->df", normed_two, d_upper, preferred_element_type=jnp.float32)
    grad_up_bias = jnp.sum(d_upper.astype(jnp.float32), axis=0)
    d_normed_two = jnp.einsum("rf,df->rd", d_upper, up_proj, preferred_element_type=jnp.float32)
    ignored, norm_two_pull = jax.vjp(layer_norm, middle, gain_two, shift_two)
    d_middle_norm, grad_gain_two, grad_shift_two = norm_two_pull(d_normed_two)
    d_middle = d_result + d_middle_norm
    d_middle_low = d_middle.astype(jnp.bfloat16)
    grad_out = jnp.einsum("rd,re->de", attended, d_middle_low, preferred_element_type=jnp.float32)
    d_attended = jnp.einsum("re,de->rd", d_middle_low, out_proj, preferred_element_type=jnp.float32)
    d_attended = d_attended.astype(jnp.bfloat16).reshape(
        sequences, tile_count, TILE, head_count, head_size
    )
    scores_again = attention_scores(query_tiles, key_window, key_pick, allowed, score_scale)
    probs = jnp.exp(scores_again - log_total)
    probs_again = probs.astype(jnp.bfloat16)
    d_probs_near = jnp.einsum(
        "spahd,spbhd->sphab", d_attended, value_window, preferred_element_type=jnp.float32
    )
    d_probs_far = jnp.einsum(
        "spahd,sphjd->sphaj", d_attended, value_pick, preferred_element_type=jnp.float32
    )
    d_probs = jnp.concatenate([d_probs_near, d_probs_far], -1)
    row_delta = jnp.sum(probs * d_probs, -1, keepdims=True)
    d_scores = (probs * (d_probs - row_delta)).astype(jnp.bfloat16)
    d_near = d_scores[..., :span]
    d_far = d_scores[..., span:]
    d_query = (
        jnp.einsum("sphab,spbhd->spahd", d_near, key_window, preferred_element_type=jnp.float32)
        + jnp.einsum("sphaj,sphjd->spahd", d_far, key_pick, preferred_element_type=jnp.float32)
    ) * score_scale
    d_key_window = (
        jnp.einsum("sphab,spahd->spbhd", d_near, query_tiles, preferred_element_type=jnp.float32)
        * score_scale
    )
    d_value_window = jnp.einsum(
        "sphab,spahd->spbhd",
        probs_again[..., :span],
        d_attended,
        preferred_element_type=jnp.float32,
    )
    d_key_pick = (
        jnp.einsum("sphaj,spahd->sphjd", d_far, query_tiles, preferred_element_type=jnp.float32)
        * score_scale
    )
    d_value_pick = jnp.einsum(
        "sphaj,spahd->sphjd",
        probs_again[..., span:],
        d_attended,
        preferred_element_type=jnp.float32,
    )
    choose_float = choose.astype(jnp.float32)
    d_key_comp = jnp.einsum(
        "sphjn,sphjd->snhd", choose_float, d_key_pick, precision=lax.Precision.HIGHEST
    )
    d_value_comp = jnp.einsum(
        "sphjn,sphjd->snhd", choose_float, d_value_pick, precision=lax.Precision.HIGHEST
    )
    d_compressed = jnp.concatenate(
        [
            d_key_comp.reshape(sequences, tile_total, model_width),
            d_value_comp.reshape(sequences, tile_total, model_width),
        ],
        -1,
    )
    own_comp = sum_at_owner(d_compressed.astype(jnp.bfloat16), "seq", 1)
    own_key_comp = own_comp[..., :model_width].reshape(
        sequences, tile_count, 1, head_count, head_size
    )
    own_value_comp = own_comp[..., model_width:].reshape(
        sequences, tile_count, 1, head_count, head_size
    )
    window_grads = jnp.stack([d_key_window, d_value_window], axis=3)
    back_part = window_grads[:, :, :TILE]
    own_part = window_grads[:, :, TILE:]
    outgoing = back_part[:, 0].reshape(sequences, TILE, 2 * model_width)
    incoming = passed_along(outgoing.astype(jnp.bfloat16), "seq", -1).astype(outgoing.dtype)
    incoming = incoming.reshape(sequences, 1, TILE, 2, head_count, head_size)
    own_total = own_part + jnp.concatenate([back_part[:, 1:], incoming], 1)
    d_key = own_total[:, :, :, 0] + tile_weights * own_key_comp / root_tile
    d_value = own_total[:, :, :, 1] + tile_weights * own_value_comp / root_tile
    d_weights = (
        jnp.sum(key_float * own_key_comp, -1) + jnp.sum(value_float * own_value_comp, -1)
    ) / root_tile
    flat_weights = weights.reshape(sequences, tile_count, TILE, head_count)
    d_logits = (
        (d_weights * flat_weights * (1.0 - flat_weights))
        .reshape(row_count, head_count)
        .astype(jnp.bfloat16)
    )
    d_packed = (
        jnp.stack([d_query, d_key, d_value], axis=3)
        .reshape(row_count, 3 * model_width)
        .astype(jnp.bfloat16)
    )
    grad_in = jnp.einsum("rd,re->de", normed, d_packed, preferred_element_type=jnp.float32)
    grad_score = jnp.einsum("rd,rh->dh", normed, d_logits, preferred_element_type=jnp.float32)
    d_normed = jnp.einsum(
        "re,de->rd", d_packed, in_proj, preferred_element_type=jnp.float32
    ) + jnp.einsum("rh,dh->rd", d_logits, scorer, preferred_element_type=jnp.float32)
    ignored_one, norm_one_pull = jax.vjp(layer_norm, hidden, gain_one, shift_one)
    d_hidden_norm, grad_gain_one, grad_shift_one = norm_one_pull(d_normed)
    grad_input = (
        (d_middle + d_hidden_norm).astype(jnp.bfloat16).reshape(sequences, tokens, model_width)
    )
    grads = (grad_in, grad_score, grad_out, grad_up, grad_up_bias, grad_down)
    columns = (grad_gain_one, grad_shift_one, grad_gain_two, grad_shift_two)
    if lax.axis_size("seq") == 8:
        return (block_out, grad_input) + reduce_all(*grads, columns)
    all_shares = (
        lax.psum_scatter(grad_in, "seq", scatter_dimension=0, tiled=True),
        lax.psum_scatter(grad_score, "seq", scatter_dimension=0, tiled=True),
        lax.psum_scatter(grad_out, "seq", scatter_dimension=0, tiled=True),
        lax.psum_scatter(grad_up, "seq", scatter_dimension=0, tiled=True),
        lax.psum_scatter(grad_up_bias, "seq", scatter_dimension=0, tiled=True),
        lax.psum_scatter(grad_down, "seq", scatter_dimension=0, tiled=True),
        lax.psum_scatter(grad_gain_one, "seq", scatter_dimension=0, tiled=True),
        lax.psum_scatter(grad_shift_one, "seq", scatter_dimension=0, tiled=True),
        lax.psum_scatter(grad_gain_two, "seq", scatter_dimension=0, tiled=True),
        lax.psum_scatter(grad_shift_two, "seq", scatter_dimension=0, tiled=True),
    )
    ordered = (
        lax.psum(all_shares[0].astype(jnp.bfloat16), "batch").astype(jnp.float32),
        lax.psum(all_shares[1].astype(jnp.bfloat16), "batch").astype(jnp.float32),
        lax.psum(all_shares[2].astype(jnp.bfloat16), "batch").astype(jnp.float32),
        lax.psum(all_shares[3].astype(jnp.bfloat16), "batch").astype(jnp.float32),
        lax.psum(all_shares[4].astype(jnp.bfloat16), "batch").astype(jnp.float32),
        lax.psum(all_shares[5].astype(jnp.bfloat16), "batch").astype(jnp.float32),
        lax.psum(all_shares[6].astype(jnp.bfloat16), "batch").astype(jnp.float32),
        lax.psum(all_shares[7].astype(jnp.bfloat16), "batch").astype(jnp.float32),
        lax.psum(all_shares[8].astype(jnp.bfloat16), "batch").astype(jnp.float32),
        lax.psum(all_shares[9].astype(jnp.bfloat16), "batch").astype(jnp.float32),
    )
    return (
        block_out,
        grad_input,
        ordered[0],
        ordered[1],
        ordered[2],
        ordered[3],
        ordered[4],
        ordered[5],
        ordered[6],
        ordered[7],
        ordered[8],
        ordered[9],
    )


def solution(mesh):
    placed = (
        P("batch", "seq", None),
        P("batch"),
        P("batch", "seq", None, None),
        P(),
        P(),
        P(),
        P(),
        P(),
        P(),
        P(),
        P(),
        P(),
        P(),
        P("batch", "seq", None),
    )
    return jax.shard_map(
        shards,
        mesh=mesh,
        in_specs=placed,
        out_specs=(
            P("batch", "seq", None),
            P("batch", "seq", None),
            P("seq", None),
            P("seq", None),
            P("seq", None),
            P("seq", None),
            P("seq"),
            P("seq", None),
            P("seq"),
            P("seq"),
            P("seq"),
            P("seq"),
        ),
        check_vma=False,
    )
```

```python
from functools import partial
import math
from types import SimpleNamespace

import jax
import jax.numpy as jnp
from jax import lax
from jax.experimental import pallas as pl
from jax.experimental.pallas import tpu as pltpu
from jax.sharding import PartitionSpec as P

TILE = 64
WIN = 64


EPS = 1e-05
NEG = -1e30
SEQ = "seq"
BATCH = "batch"


def passed_along(block, axis, distance):
    devices = range(lax.axis_size(axis))
    route = [(i - distance, i) for i in devices if i - distance in devices]
    return lax.ppermute(block, axis, route)


def cut_along(value, dim, length):
    before, after = (value.shape[:dim], value.shape[dim + 1 :])
    return jnp.moveaxis(value.reshape(*before, length, -1, *after), dim, 0)


def sum_at_owner(value, axis, dim):
    parts = cut_along(value, dim, lax.axis_size(axis))
    arrived = lax.all_to_all(parts, axis, split_axis=0, concat_axis=0, tiled=True)
    return arrived.astype(jnp.float32).sum(axis=0)


def layer_norm(values, gain, shift):
    average = jnp.mean(values, axis=-1, keepdims=True)
    centered = values - average
    variance = jnp.mean(centered * centered, axis=-1, keepdims=True)
    return centered * lax.rsqrt(variance + EPS) * gain + shift


def window_mask(tile_ids):
    row_index = lax.broadcasted_iota(jnp.int32, (TILE, 2 * TILE), 0)
    col_index = lax.broadcasted_iota(jnp.int32, (TILE, 2 * TILE), 1)
    distance = TILE + row_index - col_index
    inside = (distance >= 0) & (distance <= WIN)
    exists = (tile_ids > 0)[:, None, None] | (col_index >= TILE)[None]
    return inside[None] & exists


def allowed_mask(tile_ids, picks):
    lead = picks.shape[:3]
    near_mask = jnp.broadcast_to(window_mask(tile_ids)[None, :, None], lead + (TILE, 2 * TILE))
    far_mask = picks[:, :, :, None, :] < tile_ids[None, :, None, None, None]
    far_mask = jnp.broadcast_to(far_mask, lead + (TILE, picks.shape[3]))
    return jnp.concatenate([near_mask, far_mask], -1)


def attention_scores(query_tiles, key_window, key_pick, allowed, score_scale):
    near = jnp.einsum(
        "spahd,spbhd->sphab", query_tiles, key_window, preferred_element_type=jnp.float32
    )
    far = jnp.einsum(
        "spahd,sphjd->sphaj", query_tiles, key_pick, preferred_element_type=jnp.float32
    )
    return jnp.where(allowed, jnp.concatenate([near, far], -1) * score_scale, NEG)


MESH_ID = pl.DeviceIdType.MESH
BF = jnp.bfloat16
F32 = jnp.float32


class Place:
    def __init__(self, seq_bits):
        self.seq = lax.axis_index(SEQ)
        self.batch = lax.axis_index(BATCH)
        self.bits = {"k": self.batch % 2, "y": self.batch // 2}
        for i in range(seq_bits):
            self.bits["b%d" % i] = (self.seq // 2**i) % 2

    def partner(self, dim):
        if dim == "next":
            return (self.seq + 1, self.batch)
        if dim == "last":
            return (self.seq - 1, self.batch)
        flip = 1 - 2 * self.bits[dim]
        if dim == "k":
            return (self.seq, self.batch + flip)
        if dim == "y":
            return (self.seq, self.batch + 2 * flip)
        return (self.seq + flip * 2 ** int(dim[1:]), self.batch)

    def copy(self, src, dst, send, recv, dim):
        return pltpu.make_async_remote_copy(
            src_ref=src,
            dst_ref=dst,
            send_sem=send,
            recv_sem=recv,
            device_id=self.partner(dim),
            device_id_type=MESH_ID,
        )

    def greet(self):
        barrier = pltpu.get_barrier_semaphore()
        odd = self.bits["b0"]
        inner = jnp.where((self.seq > 0) & (self.seq < lax.axis_size(SEQ) - 1), 1, 0)
        for dim in ("k", "y", "b0", "b1", "b2"):
            pl.semaphore_signal(barrier, inc=1, device_id=self.partner(dim), device_id_type=MESH_ID)

        @pl.when(inner == 1)
        def _():
            across = (self.seq + 2 * odd - 1, self.batch)
            pl.semaphore_signal(barrier, inc=1, device_id=across, device_id_type=MESH_ID)

        pl.semaphore_wait(barrier, 5 + inner)


def pick(axes, fixed):
    return tuple(fixed[a] if a in fixed else slice(None) for a in axes)


class Flow:
    def __init__(self, place, axes, order, item, bufs, fin, send, recv):
        self.place, self.axes = place, axes
        self.dims = ("k",) + order
        self.item, self.bufs, self.fin = item, bufs, fin
        self.send, self.recv = send, recv
        self.done = 0

    def fixed(self, count):
        return {d: self.place.bits[d] for d in self.dims[:count]}

    def copy(self, j):
        bits = self.place.bits
        if j < 5:
            dim = self.dims[j]
            other = {**self.fixed(j), dim: 1 - bits[dim]}
            src, dst = self.item.at[pick(self.axes, other)], self.bufs[j]
        elif j == 5:
            dim = "y"
            src = dst = self.fin.at[bits["k"], bits["y"]]
        else:
            dim = "k"
            src = dst = self.fin.at[bits["k"]]
        return self.place.copy(src, dst, self.send.at[j], self.recv.at[j], dim)

    def add(self, j):
        fixed = self.fixed(j + 1)
        free = [a for a in self.axes if a not in fixed]
        outer = free[:-2]

        def body(i, carry):
            at = {a: (i // 2**n) % 2 for n, a in enumerate(outer)}
            here = self.item.at[pick(self.axes, {**fixed, **at})]
            total = here[...] + self.bufs[j][pick(free, at)]
            if free:
                here[...] = total
            else:
                self.fin[self.place.bits["k"], self.place.bits["y"]] = total
            return carry

        if outer:
            lax.fori_loop(0, 2 ** len(outer), body, 0)
        else:
            body(0, 0)

    def advance(self):
        j = self.done
        self.done += 1
        if j:
            self.copy(j - 1).wait_recv()
            if j <= 5:
                self.add(j - 1)
        if j < 7:
            self.copy(j).start()

    def finish(self):
        while self.done < 8:
            self.advance()
        for j in range(7):
            self.copy(j).wait_send()


KCOL = ("k", "b2", "b1", "b0", "y")
KROW = ("b2", "b1", "b0", "k", "y")
ORDERS = {"A": ("b1", "b2", "y", "b0"), "B": ("b1", "b0", "y", "b2"), "C": ("b0", "b1", "y", "b2"), "D": ("b0", "y", "b1", "b2"), "E": ("y", "b1", "b2", "b0"), "F": ("y", "b0", "b1", "b2")}
PLAN = {
    "d0": (KROW, "F", 32, 768),
    "u0": (KCOL, "A", 48, 512),
    "d1": (KROW, "E", 32, 768),
    "u1": (KCOL, "D", 48, 512),
    "d2": (KROW, "F", 32, 768),
    "u2": (KCOL, "D", 48, 512),
    "o": (KCOL, "E", 48, 384),
    "q": (KCOL, "B", 48, 384),
    "k": (KCOL, "F", 48, 384),
    "v": (KCOL, "B", 48, 384),
    "m": (KCOL, "C", 48, 128),
}
NAMES = tuple(PLAN)
SCHEDULE = (
    "",
    "",
    "",
    "0",
    "1",
    "",
    "",
    "",
    "2",
    "3",
    "01",
    "",
    "",
    "",
    "",
    "62",
    "3",
    "",
    "",
    "10",
    "",
    "2465",
    "703",
    "126",
    "8",
    "4",
    "7519023",
    "",
    "",
    "648a7659101832042a76536893a479a54784795a5889a9a",
)
FIRST = {"d0": "d0", "d1": "d1", "d2": "d0", "u0": "u0", "u1": "u1", "u2": "u0", "o": "o", "q": "q", "k": "o", "v": "q", "m": "m"}


def dot(a, b):
    return lax.dot_general(a, b, (((1,), (0,)), ((), ())), preferred_element_type=F32)


def dot_rt(a, b):
    return lax.dot_general(a, b, (((1,), (1,)), ((), ())), preferred_element_type=F32)


def dot_lt(a, b):
    return lax.dot_general(a, b, (((0,), (0,)), ((), ())), preferred_element_type=F32)


def normal(x):
    centered = x - jnp.mean(x, axis=-1, keepdims=True)
    scale = lax.rsqrt(jnp.mean(centered * centered, axis=-1, keepdims=True) + EPS)
    return centered * scale, scale


def normal_back(xhat, scale, dxhat):
    inner = jnp.mean(dxhat * xhat, axis=-1, keepdims=True)
    return scale * (dxhat - jnp.mean(dxhat, axis=-1, keepdims=True) - xhat * inner)


def heads_apart(pair):
    lane = lax.broadcasted_iota(jnp.int32, pair.shape, 1)
    zero = jnp.zeros_like(pair)
    return jnp.concatenate([jnp.where(lane < 64, pair, zero), jnp.where(lane >= 64, pair, zero)], 0)


def heads_joined(both):
    return jnp.concatenate([both[:64, :128], both[64:, 128:]], 0)


def lanes(start, size):
    return pl.ds(pl.multiple_of(start, 128), size)


HELD = pl.BlockSpec(memory_space=pl.ANY)
NEAR = pl.BlockSpec(memory_space=pltpu.VMEM)
INPUTS = dict(
    hidden=HELD,
    lengths=pl.BlockSpec(memory_space=pltpu.SMEM),
    selected=HELD,
    in_proj=HELD,
    scorer=HELD,
    out_proj=HELD,
    up_proj=HELD,
    up_bias=NEAR,
    down_proj=HELD,
    gain_one=NEAR,
    shift_one=NEAR,
    gain_two=NEAR,
    shift_two=NEAR,
    cotangent=HELD,
)


def block_shapes():
    vm = pltpu.VMEM
    shapes = dict(
        x=vm((4, 128, 768), BF),
        xh=vm((4, 64, 768), BF),
        sel=vm((4, 12, 2, 64), jnp.int32),
        win=vm((768, 2304), BF),
        wsc=vm((12, 768), BF),
        wout=vm((768, 768), BF),
        upc=vm((2, 768, 1024), BF),
        dnc=vm((2, 8, 128, 768), BF),
        t1=vm((768, 768), BF),
        t2=vm((512, 768), BF),
        h1t=vm((768, 768), BF),
        q=vm((512, 768), BF),
        kv=vm((4, 208, 1536), BF),
        pt=vm((4, 6, 208, 256), BF),
        cnt=vm((4, 6, 16, 256), F32),
        mask=vm((192, 256), F32),
        w=vm((512, 12), F32),
        wh=vm((512, 12), BF),
        wl=vm((512, 12), BF),
        spread=vm((12, 768), BF),
        dz=vm((512, 128), BF),
        co=vm((16, 768), F32),
        agb=vm((2, 2, 2, 16, 768), BF),
        ot=vm((768, 512), BF),
        m=vm((512, 768), F32),
        y=vm((512, 768), F32),
        h2t=vm((768, 512), BF),
        dyb=vm((512, 768), BF),
        dm=vm((512, 768), F32),
        g=vm((512, 1024), BF),
        gt=vm((1024, 512), BF),
        du=vm((512, 1024), BF),
        dc=vm((64, 1536), F32),
        dcb=vm((2, 2, 2, 16, 768), BF),
        rd0=vm((2, 2, 16, 768), BF),
        rd1=vm((2, 16, 768), BF),
        rd2=vm((16, 768), BF),
        hs=vm((256, 768), BF),
        hr=vm((256, 768), BF),
        sums=vm((128, 768), F32),
        bias=vm((8, 16, 128), F32),
        bias_row=vm((1, 3072), F32),
    )
    for name, (axes, order, rows, cols) in PLAN.items():
        shapes["item_" + name] = vm((2,) * 5 + (rows, cols), BF)
        for j in range(1, 5):
            shapes["buf%d_%s" % (j, name)] = vm((2,) * (4 - j) + (rows, cols), BF)
        shapes["fin_" + name] = vm((2, 2, rows, cols), BF)
    for name in dict.fromkeys(FIRST.values()):
        shapes["buf0_" + name] = vm((2,) * 4 + PLAN[name][2:], BF)
    dma = pltpu.SemaphoreType.DMA
    shapes.update(
        fsend=dma((len(NAMES), 7)),
        frecv=dma((len(NAMES), 7)),
        load=dma((8,)),
        chunk=dma((2, 9)),
        store=dma((len(NAMES) + 2,)),
        side_s=dma((8,)),
        side_r=dma((8,)),
    )
    return shapes


def block_kernel(names, *refs):
    r = SimpleNamespace(**dict(zip(names, refs)))
    place = Place(3)
    bits = place.bits
    shard = place.seq
    last_shard = lax.axis_size(SEQ) - 1

    def local(src, dst, sem):
        return pltpu.make_async_copy(src, dst, sem)

    b0, b1, b2 = bits["b0"], bits["b1"], bits["b2"]
    sources = (r.hidden, r.in_proj, r.scorer, r.selected, r.cotangent, r.out_proj)
    loads = []
    for i, (source, place_here) in enumerate(zip(sources, (r.x, r.win, r.wsc, r.sel, r.dyb, r.wout))):
        loads.append(pltpu.make_async_copy(source, place_here, r.load.at[i]))
        loads[i].start()
    x_load, win_load, wsc_load, sel_load, dyb_load, wout_load = loads

    def chunk_loads(c):
        slot = c % 2
        copies = [pltpu.make_async_copy(r.down_proj.at[:, c], r.dnc.at[slot], r.chunk.at[slot, 8])]
        for s in range(8):
            src = r.up_proj.at[:, 384 * s + 128 * c : 384 * s + 128 * c + 128]
            dst = r.upc.at[slot, :, 128 * s : 128 * s + 128]
            copies.append(pltpu.make_async_copy(src, dst, r.chunk.at[slot, s]))
        return copies

    flows = {}
    for i, name in enumerate(NAMES):
        axes, order, rows, cols = PLAN[name]
        bufs = [getattr(r, "buf0_" + FIRST[name])] + [getattr(r, "buf%d_%s" % (j, name)) for j in range(1, 5)]
        flows[name] = Flow(
            place, axes, ORDERS[order], getattr(r, "item_" + name), bufs, getattr(r, "fin_" + name), r.fsend.at[i], r.frecv.at[i]
        )

    points = iter(SCHEDULE)

    def point():
        for i in next(points):
            flows[NAMES[int(i, 16)]].advance()

    def by_column(lhs, rhs, name):
        item = flows[name].item
        out = dot(lhs, rhs).astype(BF)
        for t in range(out.shape[1] // 256):
            for k in range(2):
                half = out[:, 256 * t + 128 * k : 256 * t + 128 * k + 128]
                item[k, :, :, :, :, :, 128 * t : 128 * t + 128] = half.reshape(2, 2, 2, 2, 48, 128)
        flows[name].advance()
        point()

    place.greet()

    halo = place.copy(r.hidden.at[:, 64:128, :], r.xh, r.side_s.at[0], r.side_r.at[0], "next")

    @pl.when(shard < last_shard)
    def _():
        halo.start()

    for cp in chunk_loads(0):
        cp.start()

    g1, s1, g2, s2 = (v[...].astype(F32).reshape(1, 768) for v in (r.gain_one, r.shift_one, r.gain_two, r.shift_two))
    r.bias_row[...] = r.up_bias[...].astype(F32).reshape(1, 3072)

    r.bias[...] = jnp.zeros_like(r.bias)

    x_load.wait()

    def first_norm(s, carry):
        xhat, _ = normal(r.x[s].astype(F32))
        low = (xhat * g1 + s1).astype(BF)
        r.t1[slice(s * 128, s * 128 + 128), :] = low
        r.h1t[:, slice(s * 128, s * 128 + 128)] = low.T
        return carry

    for s in range(4):
        first_norm(s, 0)
    win_load.wait()
    wsc_load.wait()

    for i in range(2):
        out = dot(r.t1[256 * i : 256 * i + 256, :], r.win[:, 768:2304]).astype(BF)
        for s in range(2):
            r.kv[2 * i + s, 64:192, :] = out[128 * s : 128 * s + 128]
    weight = jax.nn.sigmoid(dot_rt(r.t1[0:512, :], r.wsc[...]))
    high = weight.astype(BF)
    r.w[...] = weight
    r.wh[...] = high
    r.wl[...] = (weight - high.astype(F32)).astype(BF)
    head = lax.broadcasted_iota(jnp.int32, (12, 768), 0)
    column = lax.broadcasted_iota(jnp.int32, (12, 768), 1)
    r.spread[...] = ((column >= head * 64) & (column < head * 64 + 64)).astype(F32).astype(BF)

    def spread_weight(s):
        rows = slice(128 * s, 128 * s + 128)
        return dot(r.wh[rows, :], r.spread[...]) + dot(r.wl[rows, :], r.spread[...])

    for s in range(4):
        wide = spread_weight(s)
        for part in range(2):
            values = r.kv[s, 64:192, 768 * part : 768 * part + 768].astype(F32)
            pooled = (wide * values).reshape(2, 64, 768).sum(axis=1) * 0.125
            r.co[8 * part + 2 * s : 8 * part + 2 * s + 2, :] = pooled
    r.agb[b2, b1, b0] = r.co[...].astype(BF)

    gathers = []
    for i, (dim, at) in enumerate(
        (
            ("b1", (b2, b1, b0)),
            ("b2", (b2, slice(None), b0)),
            ("b0", (slice(None), slice(None), b0)),
        )
    ):
        block = r.agb.at[at]
        gathers.append(place.copy(block, block, r.side_s.at[1 + i], r.side_r.at[1 + i], dim))
    gathers[0].start()
    r.q[...] = dot(r.t1[0:512, :], r.win[:, 0:768]).astype(BF) * jnp.asarray(0.125, BF)

    row = lax.broadcasted_iota(jnp.int32, (192, 256), 0)
    query = lax.broadcasted_iota(jnp.int32, (192, 256), 1) % 128
    inside = (row >= query) & (row <= query + 64) & ((row >= 64) | (shard > 0))
    r.mask[...] = jnp.where(inside, 0.0, NEG)
    gathers[0].wait_recv()
    gathers[1].start()
    sel_load.wait()
    own = lax.broadcasted_iota(jnp.int32, (128, 128), 0) // 64 == lax.broadcasted_iota(jnp.int32, (128, 128), 1) // 64
    own = own.astype(F32).astype(BF)
    tile_row = lax.broadcasted_iota(jnp.int32, (1, 16, 128), 1)
    before = tile_row < 2 * shard + lax.broadcasted_iota(jnp.int32, (1, 16, 128), 2) // 64
    for s in range(4):
        picks = jnp.concatenate([r.sel[s, :, 0], r.sel[s, :, 1]], axis=1)
        same = (picks[:, None, :] == tile_row).astype(F32).astype(BF)
        counts = dot(same.reshape(192, 128), own).reshape(12, 16, 128)
        counts = jnp.where(before, counts, 0.0)
        for p in range(6):
            r.cnt[s, p] = jnp.concatenate([counts[2 * p], counts[2 * p + 1]], axis=1)
    gathers[1].wait_recv()
    gathers[2].start()

    dyb_load.wait()
    in_shard = lax.broadcasted_iota(jnp.int32, (128, 768), 0) + shard * 128
    for s in range(4):
        rows = slice(128 * s, 128 * s + 128)
        keep = in_shard < r.lengths[s]
        r.dyb[rows, :] = jnp.where(keep, r.dyb[rows, :].astype(F32), 0.0).astype(BF)

    @pl.when(shard == 0)
    def _():
        r.xh[...] = jnp.zeros_like(r.xh)

    @pl.when(shard > 0)
    def _():
        halo.wait_recv()

    def halo_norm(s, carry):
        x = r.xh[2 * s : 2 * s + 2].reshape(128, 768)
        xhat, _ = normal(x.astype(F32))
        low = (xhat * g1 + s1).astype(BF)
        r.t1[slice(512 + s * 128, 640 + s * 128), :] = low
        r.h1t[:, slice(512 + s * 128, 640 + s * 128)] = low.T
        return carry

    for s in range(2):
        halo_norm(s, 0)

    out = dot(r.t1[512:768, :], r.win[:, 768:2304]).astype(BF)
    for s in range(4):
        r.kv[s, 0:64, :] = out[64 * s : 64 * s + 64]
    gathers[2].wait_recv()

    def placing(part):
        to = lax.broadcasted_iota(jnp.int32, (64, 128), 0)
        at = lax.broadcasted_iota(jnp.int32, (64, 128), 1)
        seq, tile = to // 16, to % 16
        return (at == (tile // 2) * 16 + 8 * part + 2 * seq + tile % 2).astype(F32).astype(BF)

    everything = r.agb[...].reshape(128, 768)
    for part in range(2):
        placed = dot(placing(part), everything).astype(BF)
        for s in range(4):
            r.kv[s, 192:208, 768 * part : 768 * part + 768] = placed[16 * s : 16 * s + 16]

    def pair_block(ref, p):
        return ref.at[208 * (p // 3) : 208 * (p // 3) + 208, 256 * (p % 3) : 256 * (p % 3) + 256]

    for s in range(4):
        rows = slice(s * 128, s * 128 + 128)
        for p in range(6):
            col = slice(128 * p, 128 * p + 128)
            pair_block(r.m, p)[...] = dot_rt(r.kv[s, :, col], heads_apart(r.q[rows, col]))
        for p in range(6):
            for h in range(2):
                lane = slice(128 * h, 128 * h + 128)
                scores = pair_block(r.m, p)
                count = r.cnt[s, p, :, lane]
                near = scores[:192, lane] + r.mask[:, lane]
                far = jnp.where(count > 0, scores[192:, lane], NEG)
                top = jnp.maximum(jnp.max(near, axis=0, keepdims=True), jnp.max(far, axis=0, keepdims=True))
                near = jnp.exp(near - top)
                far = count * jnp.exp(far - top)
                total = jnp.sum(near, axis=0, keepdims=True) + jnp.sum(far, axis=0, keepdims=True)
                scale = 1.0 / total
                r.pt[s, p, 0:192, lane] = (near * scale).astype(BF)
                r.pt[s, p, 192:208, lane] = (far * scale).astype(BF)
        for p in range(6):
            col = slice(128 * p, 128 * p + 128)
            values = r.kv[s, :, 768 + 128 * p : 896 + 128 * p]
            r.ot[col, rows] = heads_joined(dot_lt(values, r.pt[s, p])).astype(BF)
        r.t2[rows, :] = r.ot[:, rows].T

    wout_load.wait()

    r.m[...] = r.x[...].reshape(512, 768).astype(F32) + dot(r.t2[...], r.wout[...])

    def second_norm(s, carry):
        rows = slice(s * 128, s * 128 + 128)
        xhat, _ = normal(r.m[rows, :])
        low = (xhat * g2 + s2).astype(BF)
        r.t1[rows, :] = low
        r.h2t[:, slice(s * 128, s * 128 + 128)] = low.T
        return carry

    for s in range(4):
        second_norm(s, 0)

    for c in range(3):
        slot = c % 2
        for cp in chunk_loads(c):
            cp.wait()
        if c < 2:
            for cp in chunk_loads(c + 1):
                cp.start()
        up, down = r.upc.at[slot], r.dnc.at[slot]

        bias = jnp.concatenate([r.bias_row[:, 384 * i + 128 * c : 384 * i + 128 * c + 128] for i in range(8)], axis=1)
        root = math.sqrt(2.0 / math.pi)
        for i in range(2):
            rows = slice(256 * i, 256 * i + 256)
            u = dot(r.t1[rows, :], up[...]) + bias
            dg = dot_rt(r.dyb[rows, :], down[...].reshape(1024, 768))
            squared = u * u
            half = 0.5 + 0.5 * jnp.tanh(u * (root + root * 0.044715 * squared))
            act = u * half
            slope = half + act * (1.0 - half) * (2.0 * root + 6.0 * root * 0.044715 * squared)
            act_low = act.astype(BF)
            du = (dg * slope).astype(BF)
            r.g[rows, :] = act_low
            r.du[rows, :] = du
            r.gt[:, rows] = act_low.T
            sums = jnp.sum(du.astype(F32), axis=0, keepdims=True)
            for j in range(8):
                r.bias[j, c : c + 1, :] += sums[:, 128 * j : 128 * j + 128]
        point()

        def gradients(c=c):
            d_name = "d%d" % c
            item = flows[d_name].item
            item[...] = dot(r.gt[...], r.dyb[...]).astype(BF).reshape(2, 2, 2, 2, 2, 32, 768)
            flows[d_name].advance()
            point()
            by_column(r.h2t[...], r.du[...], "u%d" % c)

        if c < 2:
            gradients()
        dh = dot_rt(r.du[...], up[...])
        r.dm[...] = r.dm[...] + dh if c else dh
        point()
        if c < 2:
            y = dot(r.g[...], down[...].reshape(1024, 768))
            r.y[...] = (r.y if c else r.m)[...] + y
            point()

    r.sums[...] = jnp.zeros((128, 768), F32)

    def second_back(s, carry):
        rows = slice(s * 128, s * 128 + 128)
        xhat, scale = normal(r.m[rows, :])
        dh = r.dm[rows, :]
        r.sums[14:15, :] += jnp.sum(dh * xhat, axis=0, keepdims=True)
        r.sums[15:16, :] += jnp.sum(dh, axis=0, keepdims=True)
        dm = r.dyb[rows, :].astype(F32) + normal_back(xhat, scale, dh * g2)
        r.dm[rows, :] = dm
        r.t1[rows, :] = dm.astype(BF)
        return carry

    for s in range(4):
        second_back(s, 0)
    point()
    by_column(r.ot[...], r.t1[0:512, :], "o")

    r.t2[...] = dot_rt(r.t1[0:512, :], r.wout[...]).astype(BF)
    point()

    dq, dk, dv = r.upc.at[0], r.upc.at[1], r.dnc.at[1]
    for s in range(4):
        rows = slice(s * 128, s * 128 + 128)
        tiles = slice(s * 16, s * 16 + 16)
        for p in range(6):
            col = slice(128 * p, 128 * p + 128)
            pair_block(r.m, p)[...] = dot_rt(r.kv[s, :, 768 + 128 * p : 896 + 128 * p], heads_apart(r.t2[rows, col]))
        for p in range(6):
            for h in range(2):
                lane = slice(128 * h, 128 * h + 128)
                probs = r.pt[s, p, :, lane].astype(F32)
                dp = pair_block(r.m, p)[:, lane]
                delta = jnp.sum(probs * dp, axis=0, keepdims=True)
                pair_block(r.t1, p)[:, lane] = (probs * (dp - delta)).astype(BF)
        for p in range(6):
            col = slice(128 * p, 128 * p + 128)
            d_values = dot(r.pt[s, p], heads_apart(r.t2[rows, col]))
            dv[s, :, col] = d_values[64:192].astype(BF)
            dv[4 + s // 2, 64 * (s % 2) : 64 * (s % 2) + 64, col] = d_values[:64].astype(BF)
            r.dc[tiles, 768 + 128 * p : 896 + 128 * p] = d_values[192:]
        for p in range(6):
            col = slice(128 * p, 128 * p + 128)
            d_keys = dot(pair_block(r.t1, p)[...], heads_apart(r.q[rows, col]))
            dk[rows, col] = d_keys[64:192].astype(BF)
            dk[512 + s * 64 : 576 + s * 64, col] = d_keys[:64].astype(BF)
            r.dc[tiles, col] = d_keys[192:]
        for p in range(6):
            col = slice(128 * p, 128 * p + 128)
            d_query = heads_joined(dot_lt(r.kv[s, :, col], pair_block(r.t1, p)[...]))
            dq[rows, col] = (d_query.T * 0.125).astype(BF)
        if s % 2:
            point()

    sent = dot_lt(placing(0), r.dc[:, 0:768].astype(BF)) + dot_lt(placing(1), r.dc[:, 768:].astype(BF))
    r.dcb[...] = sent.astype(BF).reshape(2, 2, 2, 16, 768)
    scatters = []
    for i, (dim, at, to) in enumerate(
        (
            ("b0", (slice(None), slice(None), 1 - b0), r.rd0),
            ("b2", (1 - b2, slice(None), b0), r.rd1),
            ("b1", (b2, 1 - b1, b0), r.rd2),
        )
    ):
        scatters.append(place.copy(r.dcb.at[at], to, r.side_s.at[4 + i], r.side_r.at[4 + i], dim))
    scatters[0].start()
    point()

    out = dot_rt(dk[512:768, 0:768], r.win[:, 768:1536])
    r.hs[...] = (out + dot_rt(dv[4:6].reshape(256, 768), r.win[:, 1536:2304])).astype(BF)
    back = place.copy(r.hs, r.hr, r.side_s.at[7], r.side_r.at[7], "last")

    @pl.when(shard > 0)
    def _():
        back.start()

    point()

    gradients()
    scatters[0].wait_recv()
    for a in range(2):
        for b in range(2):
            r.dcb[a, b, b0] = r.dcb[a, b, b0] + r.rd0[a, b]
    scatters[1].start()
    by_column(r.h1t[:, 0:512], dq[0:512, 0:768], "q")
    scatters[1].wait_recv()
    for b in range(2):
        r.dcb[b2, b, b0] = r.dcb[b2, b, b0] + r.rd1[b]
    scatters[2].start()
    r.y[...] += dot(r.g[...], r.dnc[0].reshape(1024, 768))
    for s in range(4):
        rows = slice(128 * s, 128 * s + 128)
        keep = in_shard < r.lengths[s]
        r.g[rows, 0:768] = jnp.where(keep, r.y[rows, :], 0.0).astype(BF)
    out_copy = pltpu.make_async_copy(r.g.at[:, 0:768], r.block_out, r.store.at[len(NAMES)])
    out_copy.start()
    point()
    scatters[2].wait_recv()
    r.co[...] = r.dcb[b2, b1, b0].astype(F32) + r.rd2[...].astype(F32)

    r.dz[...] = jnp.zeros_like(r.dz)
    for s in range(4):
        rows = slice(128 * s, 128 * s + 128)
        wide = spread_weight(s)
        terms = jnp.zeros((128, 768), F32)
        for part in range(2):
            pair = [r.co[8 * part + 2 * s + i : 8 * part + 2 * s + i + 1, :] for i in range(2)]
            grad = jnp.concatenate([jnp.broadcast_to(row, (64, 768)) for row in pair], axis=0) * 0.125
            terms += r.kv[s, 64:192, 768 * part : 768 * part + 768].astype(F32) * grad
            if part == 0:
                dk[rows, 0:768] = (dk[rows, 0:768].astype(F32) + wide * grad).astype(BF)
            else:
                dv[s] = (dv[s].astype(F32) + wide * grad).astype(BF)
        high = terms.astype(BF)
        low = (terms - high.astype(F32)).astype(BF)
        d_weight = dot_rt(high, r.spread[...]) + dot_rt(low, r.spread[...])
        weight = r.w[rows, :]
        r.dz[rows, 0:12] = (d_weight * weight * (1.0 - weight)).astype(BF)
    point()

    by_column(r.h1t[...], dk[:, 0:768], "k")
    by_column(r.h1t[...], dv[0:6].reshape(768, 768), "v")

    out = dot_rt(dq[0:512, 0:768], r.win[:, 0:768])
    out += dot_rt(dk[0:512, 0:768], r.win[:, 768:1536])
    out += dot_rt(dv[0:4].reshape(512, 768), r.win[:, 1536:2304])
    r.m[...] = out + dot(r.dz[:, 0:12], r.wsc[...])
    point()

    @pl.when(shard == last_shard)
    def _():
        r.hr[...] = jnp.zeros_like(r.hr)

    @pl.when(shard < last_shard)
    def _():
        back.wait_recv()

    def first_back(s, carry):
        rows = slice(s * 128, s * 128 + 128)
        xhat, scale = normal(r.x[s].astype(F32))
        from_next = r.hr[s * 64 : s * 64 + 64, :].astype(F32)
        dh = r.m[rows, :] + jnp.concatenate([jnp.zeros((64, 768), F32), from_next], axis=0)
        r.sums[12:13, :] += jnp.sum(dh * xhat, axis=0, keepdims=True)
        r.sums[13:14, :] += jnp.sum(dh, axis=0, keepdims=True)
        r.t2[rows, :] = (r.dm[rows, :] + normal_back(xhat, scale, dh * g1)).astype(BF)
        return carry

    for s in range(4):
        first_back(s, 0)
    grad_copy = pltpu.make_async_copy(r.t2, r.grad_input, r.store.at[len(NAMES) + 1])
    grad_copy.start()
    point()

    item = flows["m"].item
    left = dot(r.h1t[:, 0:512], r.dz[...]) + r.sums[...].T
    item[0] = left.astype(BF).reshape(2, 2, 2, 2, 48, 128)
    item[1] = jnp.zeros((2, 2, 2, 2, 48, 128), BF)
    for s in range(8):
        item[1, s // 4, (s // 2) % 2, s % 2, 0, 0:16, :] = r.bias[s].astype(BF)
    flows["m"].advance()
    point()

    stores = [pltpu.make_async_copy(getattr(r, "fin_" + name), getattr(r, "out_" + name), r.store.at[i]) for i, name in enumerate(NAMES)]
    stored = set()

    def store():
        for i, name in enumerate(NAMES):
            if flows[name].done == 8 and i not in stored:
                stored.add(i)
                stores[i].start()

    store()
    for i in next(points):
        flows[NAMES[int(i, 16)]].advance()
        store()
    for i, name in enumerate(NAMES):
        flows[name].finish()
        store()
    for cp in stores:
        cp.wait()
    out_copy.wait()
    grad_copy.wait()

    @pl.when(shard < last_shard)
    def _():
        halo.wait_send()

    @pl.when(shard > 0)
    def _():
        back.wait_send()

    for cp in gathers + scatters:
        cp.wait_send()


def finish_kernel(names, *refs):
    r = SimpleNamespace(**dict(zip(names, refs)))
    copies = []
    rows_in = (pltpu.make_async_copy(r.block, r.rows.at[0], r.sems.at[0]), pltpu.make_async_copy(r.grad, r.rows.at[1], r.sems.at[1]))
    loads = {}
    for i, name in enumerate(NAMES):
        loads[name] = pltpu.make_async_copy(getattr(r, "sum_" + name), getattr(r, "fin_" + name), r.sems.at[2 + i])
    for cp in rows_in + tuple(loads.values()):
        cp.start()

    def columns(name, to, place):
        rows, cols = PLAN[name][2:]
        loads[name].wait()
        fin = getattr(r, "fin_" + name)
        for k in range(2):
            for y in range(2):
                for t in range(cols // 128):
                    at = place(2 * t + k)
                    to[48 * y : 48 * y + 48, at : at + 128] = fin[k, y, :, 128 * t : 128 * t + 128].astype(F32)

    def store(src, dst):
        copies.append(pltpu.make_async_copy(src, dst, r.sems.at[2 + len(NAMES) + len(copies)]))
        copies[-1].start()

    for cp, src, dst in zip(rows_in, (r.rows.at[0], r.rows.at[1]), (r.block_out, r.grad_input)):
        cp.wait()
        store(src, dst)
    for c in range(3):
        name = "d%d" % c
        loads[name].wait()
        r.down[128 * c : 128 * c + 128, :] = getattr(r, "fin_" + name)[...].reshape(128, 768).astype(F32)
        columns("u%d" % c, r.up, lambda i, c=c: 384 * i + 128 * c)
    store(r.down, r.grad_down)
    store(r.up, r.grad_up)
    columns("o", r.out, lambda i: 128 * i)
    store(r.out, r.grad_out)
    for g, name in enumerate("qkv"):
        columns(name, r.into, lambda i, g=g: 768 * g + 128 * i)
    store(r.into, r.grad_in)
    loads["m"].wait()
    left = jnp.concatenate([r.fin_m[0, 0], r.fin_m[0, 1]], axis=0).astype(F32).T
    r.score[...] = left[0:12]
    for i, gain in enumerate((r.grad_gain_one, r.grad_shift_one, r.grad_gain_two, r.grad_shift_two)):
        gain[...] = left[12 + i : 13 + i].reshape(96)
    rows = r.fin_m[1, 0].astype(F32)
    for c in range(3):
        r.grad_bias[128 * c : 128 * c + 128] = rows[c : c + 1].reshape(128)
    for cp in copies:
        cp.wait()


def fits(hidden_in, selected, scorer, up_proj):
    sizes = (hidden_in.shape, selected.shape, scorer.shape, up_proj.shape)
    wanted = ((4, 128, 768), (4, 2, 12, 64), (768, 12), (768, 3072))
    return sizes == wanted and (lax.axis_size(SEQ), lax.axis_size(BATCH)) == (8, 4)


def fused(
    hidden_in,
    lengths,
    selected,
    in_proj,
    scorer,
    out_proj,
    up_proj,
    up_bias,
    down_proj,
    first_gain,
    first_shift,
    second_gain,
    second_shift,
    cotangent,
):
    scratch = block_shapes()
    fins = tuple("out_" + name for name in NAMES)
    names = tuple(INPUTS) + ("block_out", "grad_input") + fins + tuple(scratch)
    piece_shapes = [(2, 2) + PLAN[name][2:] for name in NAMES]
    inputs = dict(
        hidden=hidden_in,
        lengths=lengths,
        selected=jnp.transpose(selected, (0, 2, 1, 3)),
        in_proj=in_proj,
        scorer=scorer.T,
        out_proj=out_proj,
        up_proj=up_proj,
        up_bias=up_bias,
        down_proj=down_proj.reshape(8, 3, 128, 768),
        gain_one=first_gain,
        shift_one=first_shift,
        gain_two=second_gain,
        shift_two=second_shift,
        cotangent=cotangent.reshape(512, 768),
    )
    block_out, grad_input, *sums = pl.pallas_call(
        partial(block_kernel, names),
        out_shape=[jax.ShapeDtypeStruct(shape, BF) for shape in [(512, 768)] * 2 + piece_shapes],
        in_specs=[INPUTS[name] for name in INPUTS],
        out_specs=[HELD] * (2 + len(NAMES)),
        scratch_shapes=list(scratch.values()),
        compiler_params=pltpu.CompilerParams(
            collective_id=0, has_side_effects=True, vmem_limit_bytes=64 * 2**20 - 65536
        ),
        name="block",
    )(*(inputs[name] for name in INPUTS))
    outs = dict(
        block_out=((512, 768), BF, HELD),
        grad_input=((512, 768), BF, HELD),
        grad_in=((96, 2304), F32, HELD),
        score=((12, 96), F32, NEAR),
        grad_out=((96, 768), F32, HELD),
        grad_up=((96, 3072), F32, HELD),
        grad_bias=((384,), F32, NEAR),
        grad_down=((384, 768), F32, HELD),
        grad_gain_one=((96,), F32, NEAR),
        grad_shift_one=((96,), F32, NEAR),
        grad_gain_two=((96,), F32, NEAR),
        grad_shift_two=((96,), F32, NEAR),
    )
    scratch = {"fin_" + name: pltpu.VMEM(shape, BF) for name, shape in zip(NAMES, piece_shapes)}
    scratch.update(
        rows=pltpu.VMEM((2, 512, 768), BF),
        into=pltpu.VMEM((96, 2304), F32),
        out=pltpu.VMEM((96, 768), F32),
        up=pltpu.VMEM((96, 3072), F32),
        down=pltpu.VMEM((384, 768), F32),
        sems=pltpu.SemaphoreType.DMA((len(NAMES) + 8,)),
    )
    names = ("block", "grad") + tuple("sum_" + name for name in NAMES) + tuple(outs) + tuple(scratch)
    block_out, grad_input, grad_in, score, *rest = pl.pallas_call(
        partial(finish_kernel, names),
        out_shape=[jax.ShapeDtypeStruct(shape, kind) for shape, kind, spec in outs.values()],
        in_specs=[HELD] * (2 + len(NAMES)),
        out_specs=[spec for shape, kind, spec in outs.values()],
        scratch_shapes=list(scratch.values()),
        compiler_params=pltpu.CompilerParams(vmem_limit_bytes=64 * 2**20 - 65536),
        name="finish",
    )(block_out, grad_input, *sums)
    return (block_out.reshape(4, 128, 768), grad_input.reshape(4, 128, 768), grad_in, score.T, *rest)


def shards(
    hidden_in,
    lengths,
    selected,
    in_proj,
    scorer,
    out_proj,
    up_proj,
    up_bias,
    down_proj,
    first_gain,
    first_shift,
    second_gain,
    second_shift,
    cotangent,
):
    if fits(hidden_in, selected, scorer, up_proj):
        return fused(
            hidden_in,
            lengths,
            selected,
            in_proj,
            scorer,
            out_proj,
            up_proj,
            up_bias,
            down_proj,
            first_gain,
            first_shift,
            second_gain,
            second_shift,
            cotangent,
        )
    sequences, tokens, model_width = hidden_in.shape
    head_count = scorer.shape[1]
    head_size = model_width // head_count
    tile_count = tokens // TILE
    row_count = sequences * tokens
    span = 2 * TILE
    score_scale = 1.0 / math.sqrt(head_size)
    root_tile = math.sqrt(TILE)
    gain_one = first_gain.astype(jnp.float32)
    shift_one = first_shift.astype(jnp.float32)
    gain_two = second_gain.astype(jnp.float32)
    shift_two = second_shift.astype(jnp.float32)
    hidden = hidden_in.astype(jnp.float32).reshape(row_count, model_width)
    normed = layer_norm(hidden, gain_one, shift_one).astype(jnp.bfloat16)
    packed = jnp.dot(normed, in_proj, preferred_element_type=jnp.float32).astype(jnp.bfloat16)
    weights = jax.nn.sigmoid(jnp.dot(normed, scorer, preferred_element_type=jnp.float32))
    shaped = packed.reshape(sequences, tile_count, TILE, 3, head_count, head_size)
    query_tiles = shaped[:, :, :, 0]
    pair_tiles = shaped[:, :, :, 1:]
    key_float = pair_tiles[:, :, :, 0].astype(jnp.float32)
    value_float = pair_tiles[:, :, :, 1].astype(jnp.float32)
    tile_weights = weights.reshape(sequences, tile_count, TILE, head_count, 1)
    key_comp = jnp.sum(tile_weights * key_float, axis=2) / root_tile
    value_comp = jnp.sum(tile_weights * value_float, axis=2) / root_tile
    compressed = jnp.concatenate(
        [
            key_comp.reshape(sequences, tile_count, model_width),
            value_comp.reshape(sequences, tile_count, model_width),
        ],
        -1,
    ).astype(jnp.bfloat16)
    gathered = lax.all_gather(compressed, SEQ, axis=1, tiled=True)
    last_rows = packed.reshape(sequences, tokens, 3 * model_width)[:, tokens - TILE :, model_width:]
    previous = passed_along(last_rows, SEQ, 1)
    previous = previous.reshape(sequences, 1, TILE, 2, head_count, head_size)
    before = jnp.concatenate([previous, pair_tiles[:, :-1]], 1)
    window_pairs = jnp.concatenate([before, pair_tiles], 2)
    key_window = window_pairs[:, :, :, 0]
    value_window = window_pairs[:, :, :, 1]
    tile_total = gathered.shape[1]
    choose = (selected[..., None] == jnp.arange(tile_total, dtype=jnp.int32)).astype(jnp.bfloat16)
    gathered_split = gathered.reshape(sequences, tile_total, 2, head_count, head_size)
    key_pick = jnp.einsum(
        "sphjn,snhd->sphjd", choose, gathered_split[:, :, 0], preferred_element_type=jnp.float32
    ).astype(jnp.bfloat16)
    value_pick = jnp.einsum(
        "sphjn,snhd->sphjd", choose, gathered_split[:, :, 1], preferred_element_type=jnp.float32
    ).astype(jnp.bfloat16)
    tile_ids = lax.axis_index(SEQ) * tile_count + jnp.arange(tile_count, dtype=jnp.int32)
    allowed = allowed_mask(tile_ids, selected)
    scores = attention_scores(query_tiles, key_window, key_pick, allowed, score_scale)
    top_score = jnp.max(scores, -1, keepdims=True)
    log_total = top_score + jnp.log(jnp.sum(jnp.exp(scores - top_score), -1, keepdims=True))
    probs_low = jnp.exp(scores - log_total).astype(jnp.bfloat16)
    near_out = jnp.einsum(
        "sphab,spbhd->spahd",
        probs_low[..., :span],
        value_window,
        preferred_element_type=jnp.float32,
    )
    far_out = jnp.einsum(
        "sphaj,sphjd->spahd", probs_low[..., span:], value_pick, preferred_element_type=jnp.float32
    )
    attended = (near_out + far_out).reshape(row_count, model_width).astype(jnp.bfloat16)
    middle = hidden + jnp.dot(attended, out_proj, preferred_element_type=jnp.float32)
    normed_two = layer_norm(middle, gain_two, shift_two).astype(jnp.bfloat16)
    upper = jnp.dot(normed_two, up_proj, preferred_element_type=jnp.float32) + up_bias.astype(
        jnp.float32
    )
    gelu_fn = partial(jax.nn.gelu, approximate=True)
    active, gelu_pull = jax.vjp(gelu_fn, upper)
    active = active.astype(jnp.bfloat16)
    result = middle + jnp.dot(active, down_proj, preferred_element_type=jnp.float32)
    positions = lax.axis_index(SEQ) * tokens + jnp.arange(tokens, dtype=jnp.int32)
    valid = (positions[None, :] < lengths[:, None]).reshape(row_count, 1)
    block_out = (
        jnp.where(valid, result, 0.0).astype(jnp.bfloat16).reshape(sequences, tokens, model_width)
    )
    d_result = jnp.where(valid, cotangent.astype(jnp.float32).reshape(row_count, model_width), 0.0)
    d_result_low = d_result.astype(jnp.bfloat16)
    grad_down = jnp.einsum("rf,rd->fd", active, d_result_low, preferred_element_type=jnp.float32)
    d_active = jnp.einsum("rd,fd->rf", d_result_low, down_proj, preferred_element_type=jnp.float32)
    d_upper = gelu_pull(d_active)[0].astype(jnp.bfloat16)
    grad_up = jnp.einsum("rd,rf->df", normed_two, d_upper, preferred_element_type=jnp.float32)
    grad_up_bias = jnp.sum(d_upper.astype(jnp.float32), axis=0)
    d_normed_two = jnp.einsum("rf,df->rd", d_upper, up_proj, preferred_element_type=jnp.float32)
    ignored, norm_two_pull = jax.vjp(layer_norm, middle, gain_two, shift_two)
    d_middle_norm, grad_gain_two, grad_shift_two = norm_two_pull(d_normed_two)
    d_middle = d_result + d_middle_norm
    d_middle_low = d_middle.astype(jnp.bfloat16)
    grad_out = jnp.einsum("rd,re->de", attended, d_middle_low, preferred_element_type=jnp.float32)
    d_attended = jnp.einsum("re,de->rd", d_middle_low, out_proj, preferred_element_type=jnp.float32)
    d_attended = d_attended.astype(jnp.bfloat16).reshape(
        sequences, tile_count, TILE, head_count, head_size
    )
    scores_again = attention_scores(query_tiles, key_window, key_pick, allowed, score_scale)
    probs = jnp.exp(scores_again - log_total)
    probs_again = probs.astype(jnp.bfloat16)
    d_probs_near = jnp.einsum(
        "spahd,spbhd->sphab", d_attended, value_window, preferred_element_type=jnp.float32
    )
    d_probs_far = jnp.einsum(
        "spahd,sphjd->sphaj", d_attended, value_pick, preferred_element_type=jnp.float32
    )
    d_probs = jnp.concatenate([d_probs_near, d_probs_far], -1)
    row_delta = jnp.sum(probs * d_probs, -1, keepdims=True)
    d_scores = (probs * (d_probs - row_delta)).astype(jnp.bfloat16)
    d_near = d_scores[..., :span]
    d_far = d_scores[..., span:]
    d_query = (
        jnp.einsum("sphab,spbhd->spahd", d_near, key_window, preferred_element_type=jnp.float32)
        + jnp.einsum("sphaj,sphjd->spahd", d_far, key_pick, preferred_element_type=jnp.float32)
    ) * score_scale
    d_key_window = (
        jnp.einsum("sphab,spahd->spbhd", d_near, query_tiles, preferred_element_type=jnp.float32)
        * score_scale
    )
    d_value_window = jnp.einsum(
        "sphab,spahd->spbhd",
        probs_again[..., :span],
        d_attended,
        preferred_element_type=jnp.float32,
    )
    d_key_pick = (
        jnp.einsum("sphaj,spahd->sphjd", d_far, query_tiles, preferred_element_type=jnp.float32)
        * score_scale
    )
    d_value_pick = jnp.einsum(
        "sphaj,spahd->sphjd",
        probs_again[..., span:],
        d_attended,
        preferred_element_type=jnp.float32,
    )
    choose_float = choose.astype(jnp.float32)
    d_key_comp = jnp.einsum(
        "sphjn,sphjd->snhd", choose_float, d_key_pick, precision=lax.Precision.HIGHEST
    )
    d_value_comp = jnp.einsum(
        "sphjn,sphjd->snhd", choose_float, d_value_pick, precision=lax.Precision.HIGHEST
    )
    d_compressed = jnp.concatenate(
        [
            d_key_comp.reshape(sequences, tile_total, model_width),
            d_value_comp.reshape(sequences, tile_total, model_width),
        ],
        -1,
    )
    own_comp = sum_at_owner(d_compressed.astype(jnp.bfloat16), SEQ, 1)
    own_key_comp = own_comp[..., :model_width].reshape(
        sequences, tile_count, 1, head_count, head_size
    )
    own_value_comp = own_comp[..., model_width:].reshape(
        sequences, tile_count, 1, head_count, head_size
    )
    window_grads = jnp.stack([d_key_window, d_value_window], axis=3)
    back_part = window_grads[:, :, :TILE]
    own_part = window_grads[:, :, TILE:]
    outgoing = back_part[:, 0].reshape(sequences, TILE, 2 * model_width)
    incoming = passed_along(outgoing.astype(jnp.bfloat16), SEQ, -1).astype(outgoing.dtype)
    incoming = incoming.reshape(sequences, 1, TILE, 2, head_count, head_size)
    own_total = own_part + jnp.concatenate([back_part[:, 1:], incoming], 1)
    d_key = own_total[:, :, :, 0] + tile_weights * own_key_comp / root_tile
    d_value = own_total[:, :, :, 1] + tile_weights * own_value_comp / root_tile
    d_weights = (
        jnp.sum(key_float * own_key_comp, -1) + jnp.sum(value_float * own_value_comp, -1)
    ) / root_tile
    flat_weights = weights.reshape(sequences, tile_count, TILE, head_count)
    d_logits = (
        (d_weights * flat_weights * (1.0 - flat_weights))
        .reshape(row_count, head_count)
        .astype(jnp.bfloat16)
    )
    d_packed = (
        jnp.stack([d_query, d_key, d_value], axis=3)
        .reshape(row_count, 3 * model_width)
        .astype(jnp.bfloat16)
    )
    grad_in = jnp.einsum("rd,re->de", normed, d_packed, preferred_element_type=jnp.float32)
    grad_score = jnp.einsum("rd,rh->dh", normed, d_logits, preferred_element_type=jnp.float32)
    d_normed = jnp.einsum(
        "re,de->rd", d_packed, in_proj, preferred_element_type=jnp.float32
    ) + jnp.einsum("rh,dh->rd", d_logits, scorer, preferred_element_type=jnp.float32)
    ignored_one, norm_one_pull = jax.vjp(layer_norm, hidden, gain_one, shift_one)
    d_hidden_norm, grad_gain_one, grad_shift_one = norm_one_pull(d_normed)
    grad_input = (
        (d_middle + d_hidden_norm).astype(jnp.bfloat16).reshape(sequences, tokens, model_width)
    )
    all_shares = (
        lax.psum_scatter(grad_in, SEQ, scatter_dimension=0, tiled=True),
        lax.psum_scatter(grad_score, SEQ, scatter_dimension=0, tiled=True),
        lax.psum_scatter(grad_out, SEQ, scatter_dimension=0, tiled=True),
        lax.psum_scatter(grad_up, SEQ, scatter_dimension=0, tiled=True),
        lax.psum_scatter(grad_up_bias, SEQ, scatter_dimension=0, tiled=True),
        lax.psum_scatter(grad_down, SEQ, scatter_dimension=0, tiled=True),
        lax.psum_scatter(grad_gain_one, SEQ, scatter_dimension=0, tiled=True),
        lax.psum_scatter(grad_shift_one, SEQ, scatter_dimension=0, tiled=True),
        lax.psum_scatter(grad_gain_two, SEQ, scatter_dimension=0, tiled=True),
        lax.psum_scatter(grad_shift_two, SEQ, scatter_dimension=0, tiled=True),
    )
    ordered = (
        lax.psum(all_shares[0].astype(jnp.bfloat16), BATCH).astype(jnp.float32),
        lax.psum(all_shares[1].astype(jnp.bfloat16), BATCH).astype(jnp.float32),
        lax.psum(all_shares[2].astype(jnp.bfloat16), BATCH).astype(jnp.float32),
        lax.psum(all_shares[3].astype(jnp.bfloat16), BATCH).astype(jnp.float32),
        lax.psum(all_shares[4].astype(jnp.bfloat16), BATCH).astype(jnp.float32),
        lax.psum(all_shares[5].astype(jnp.bfloat16), BATCH).astype(jnp.float32),
        lax.psum(all_shares[6].astype(jnp.bfloat16), BATCH).astype(jnp.float32),
        lax.psum(all_shares[7].astype(jnp.bfloat16), BATCH).astype(jnp.float32),
        lax.psum(all_shares[8].astype(jnp.bfloat16), BATCH).astype(jnp.float32),
        lax.psum(all_shares[9].astype(jnp.bfloat16), BATCH).astype(jnp.float32),
    )
    return (
        block_out,
        grad_input,
        ordered[0],
        ordered[1],
        ordered[2],
        ordered[3],
        ordered[4],
        ordered[5],
        ordered[6],
        ordered[7],
        ordered[8],
        ordered[9],
    )


def solution(mesh):
    placed = (
        P(BATCH, SEQ, None),
        P(BATCH),
        P(BATCH, SEQ, None, None),
        P(),
        P(),
        P(),
        P(),
        P(),
        P(),
        P(),
        P(),
        P(),
        P(),
        P(BATCH, SEQ, None),
    )
    return jax.shard_map(
        shards,
        mesh=mesh,
        in_specs=placed,
        out_specs=(
            P(BATCH, SEQ, None),
            P(BATCH, SEQ, None),
            P(SEQ, None),
            P(SEQ, None),
            P(SEQ, None),
            P(SEQ, None),
            P(SEQ),
            P(SEQ, None),
            P(SEQ),
            P(SEQ),
            P(SEQ),
            P(SEQ),
        ),
        check_vma=False,
    )
```

```python
from functools import partial
import math
from types import SimpleNamespace

import jax
import jax.numpy as jnp
from jax import lax
from jax.experimental import pallas as pl
from jax.experimental.pallas import tpu as pltpu
from jax.sharding import PartitionSpec as P

TILE = 64
WIN = 64


EPS = 1e-05
NEG = -1e30
SEQ = "seq"
BATCH = "batch"


def passed_along(block, axis, distance):
    devices = range(lax.axis_size(axis))
    route = [(i - distance, i) for i in devices if i - distance in devices]
    return lax.ppermute(block, axis, route)


def cut_along(value, dim, length):
    before, after = (value.shape[:dim], value.shape[dim + 1 :])
    return jnp.moveaxis(value.reshape(*before, length, -1, *after), dim, 0)


def sum_at_owner(value, axis, dim):
    parts = cut_along(value, dim, lax.axis_size(axis))
    arrived = lax.all_to_all(parts, axis, split_axis=0, concat_axis=0, tiled=True)
    return arrived.astype(jnp.float32).sum(axis=0)


def layer_norm(values, gain, shift):
    average = jnp.mean(values, axis=-1, keepdims=True)
    centered = values - average
    variance = jnp.mean(centered * centered, axis=-1, keepdims=True)
    return centered * lax.rsqrt(variance + EPS) * gain + shift


def window_mask(tile_ids):
    row_index = lax.broadcasted_iota(jnp.int32, (TILE, 2 * TILE), 0)
    col_index = lax.broadcasted_iota(jnp.int32, (TILE, 2 * TILE), 1)
    distance = TILE + row_index - col_index
    inside = (distance >= 0) & (distance <= WIN)
    exists = (tile_ids > 0)[:, None, None] | (col_index >= TILE)[None]
    return inside[None] & exists


def allowed_mask(tile_ids, picks):
    lead = picks.shape[:3]
    near_mask = jnp.broadcast_to(window_mask(tile_ids)[None, :, None], lead + (TILE, 2 * TILE))
    far_mask = picks[:, :, :, None, :] < tile_ids[None, :, None, None, None]
    far_mask = jnp.broadcast_to(far_mask, lead + (TILE, picks.shape[3]))
    return jnp.concatenate([near_mask, far_mask], -1)


def attention_scores(query_tiles, key_window, key_pick, allowed, score_scale):
    near = jnp.einsum(
        "spahd,spbhd->sphab", query_tiles, key_window, preferred_element_type=jnp.float32
    )
    far = jnp.einsum(
        "spahd,sphjd->sphaj", query_tiles, key_pick, preferred_element_type=jnp.float32
    )
    return jnp.where(allowed, jnp.concatenate([near, far], -1) * score_scale, NEG)


MESH_ID = pl.DeviceIdType.MESH
BF = jnp.bfloat16
F32 = jnp.float32


class Place:
    def __init__(self, seq_bits):
        self.seq = lax.axis_index(SEQ)
        self.batch = lax.axis_index(BATCH)
        self.bits = {"k": self.batch % 2, "y": self.batch // 2}
        for i in range(seq_bits):
            self.bits["b%d" % i] = (self.seq // 2**i) % 2

    def partner(self, dim):
        if isinstance(dim, int):
            return (self.seq + dim, self.batch)
        flip = 1 - 2 * self.bits[dim]
        if dim == "k":
            return (self.seq, self.batch + flip)
        if dim == "y":
            return (self.seq, self.batch + 2 * flip)
        return (self.seq + flip * 2 ** int(dim[1:]), self.batch)

    def copy(self, src, dst, send, recv, dim):
        return pltpu.make_async_remote_copy(
            src_ref=src,
            dst_ref=dst,
            send_sem=send,
            recv_sem=recv,
            device_id=self.partner(dim),
            device_id_type=MESH_ID,
        )

    def greet(self):
        barrier = pltpu.get_barrier_semaphore()
        count = lax.axis_size(SEQ)
        others = [((self.seq + i) % count, self.batch) for i in range(1, count)]
        others += [self.partner("k"), self.partner("y")]
        for other in others:
            pl.semaphore_signal(barrier, inc=1, device_id=other, device_id_type=MESH_ID)
        pl.semaphore_wait(barrier, len(others))


def pick(axes, fixed):
    return tuple(fixed[a] if a in fixed else slice(None) for a in axes)


class Flow:
    def __init__(self, place, axes, order, item, bufs, fin, send, recv):
        self.place, self.axes = place, axes
        self.dims = ("k",) + order
        self.item, self.bufs, self.fin = item, bufs, fin
        self.send, self.recv = send, recv
        self.done = 0

    def fixed(self, count):
        return {d: self.place.bits[d] for d in self.dims[:count]}

    def copy(self, j):
        bits = self.place.bits
        if j < 5:
            dim = self.dims[j]
            other = {**self.fixed(j), dim: 1 - bits[dim]}
            src, dst = self.item.at[pick(self.axes, other)], self.bufs[j]
        elif j == 5:
            dim = "y"
            src = dst = self.fin.at[bits["k"], bits["y"]]
        else:
            dim = "k"
            src = dst = self.fin.at[bits["k"]]
        return self.place.copy(src, dst, self.send.at[j], self.recv.at[j], dim)

    def add(self, j):
        fixed = self.fixed(j + 1)
        free = [a for a in self.axes if a not in fixed]
        outer = free[:-2]

        def body(i, carry):
            at = {a: (i // 2**n) % 2 for n, a in enumerate(outer)}
            here = self.item.at[pick(self.axes, {**fixed, **at})]
            total = here[...] + self.bufs[j][pick(free, at)]
            if free:
                here[...] = total
            else:
                self.fin[self.place.bits["k"], self.place.bits["y"]] = total
            return carry

        if outer:
            lax.fori_loop(0, 2 ** len(outer), body, 0)
        else:
            body(0, 0)

    def advance(self):
        j = self.done
        self.done += 1
        if j:
            self.copy(j - 1).wait_recv()
            if j <= 5:
                self.add(j - 1)
        if j < 7:
            self.copy(j).start()

    def finish(self):
        while self.done < 8:
            self.advance()
        for j in range(7):
            self.copy(j).wait_send()


KCOL = ("k", "b2", "b1", "b0", "y")
KROW = ("b2", "b1", "b0", "k", "y")
ORDERS = {"A": ("b1", "b2", "y", "b0"), "B": ("b0", "b1", "b2", "y"), "C": ("b0", "y", "b1", "b2"), "D": ("y", "b1", "b2", "b0"), "E": ("y", "b1", "b0", "b2")}
PLAN = {
    "d0": (KROW, "A", 32, 768),
    "u0": (KCOL, "D", 48, 512),
    "d1": (KROW, "D", 32, 768),
    "u1": (KCOL, "C", 48, 512),
    "d2": (KROW, "B", 32, 768),
    "u2": (KCOL, "D", 48, 512),
    "o": (KCOL, "D", 48, 384),
    "q": (KCOL, "C", 48, 384),
    "k": (KCOL, "C", 48, 384),
    "v": (KCOL, "E", 48, 384),
    "m": (KCOL, "D", 16, 128),
}
NAMES = tuple(PLAN)
SCHEDULE = (
    "",
    "",
    "",
    "0",
    "1",
    "",
    "",
    "",
    "2",
    "3",
    "0",
    "1",
    "",
    "",
    "",
    "6",
    "",
    "",
    "32",
    "",
    "4015",
    "76",
    "2",
    "83",
    "016",
    "49",
    "23",
    "",
    "",
    "576a43980517a343980107af54126897a5424862a9765758"
    "a8a99",
)
FIRST = {"d0": "d0", "d1": "d1", "d2": "d0", "u0": "u0", "u1": "u1", "u2": "u0", "o": "o", "q": "q", "k": "o", "v": "q", "m": "m"}


def dot(a, b):
    return lax.dot_general(a, b, (((1,), (0,)), ((), ())), preferred_element_type=F32)


def dot_rt(a, b):
    return lax.dot_general(a, b, (((1,), (1,)), ((), ())), preferred_element_type=F32)


def dot_lt(a, b):
    return lax.dot_general(a, b, (((0,), (0,)), ((), ())), preferred_element_type=F32)


def normal(x):
    centered = x - jnp.mean(x, axis=-1, keepdims=True)
    scale = lax.rsqrt(jnp.mean(centered * centered, axis=-1, keepdims=True) + EPS)
    return centered * scale, scale


def normal_back(xhat, scale, dxhat):
    inner = jnp.mean(dxhat * xhat, axis=-1, keepdims=True)
    return scale * (dxhat - jnp.mean(dxhat, axis=-1, keepdims=True) - xhat * inner)


def heads_apart(pair):
    lane = lax.broadcasted_iota(jnp.int32, pair.shape, 1)
    zero = jnp.zeros_like(pair)
    return jnp.concatenate([jnp.where(lane < 64, pair, zero), jnp.where(lane >= 64, pair, zero)], 0)


def heads_joined(both):
    return jnp.concatenate([both[:64, :128], both[64:, 128:]], 0)


def lanes(start, size):
    return pl.ds(pl.multiple_of(start, 128), size)


HELD = pl.BlockSpec(memory_space=pl.ANY)
NEAR = pl.BlockSpec(memory_space=pltpu.VMEM)
INPUTS = dict(
    hidden=HELD,
    lengths=pl.BlockSpec(memory_space=pltpu.SMEM),
    selected=HELD,
    in_proj=HELD,
    scorer=HELD,
    out_proj=HELD,
    up_proj=HELD,
    up_bias=NEAR,
    down_proj=HELD,
    gain_one=NEAR,
    shift_one=NEAR,
    gain_two=NEAR,
    shift_two=NEAR,
    cotangent=HELD,
)


def block_shapes():
    vm = pltpu.VMEM
    shapes = dict(
        x=vm((4, 128, 768), BF),
        xh=vm((4, 64, 768), BF),
        sel=vm((4, 12, 2, 64), jnp.int32),
        win=vm((768, 2304), BF),
        wsc=vm((12, 768), BF),
        wout=vm((768, 768), BF),
        upc=vm((2, 768, 1024), BF),
        dnc=vm((2, 8, 128, 768), BF),
        t1=vm((768, 768), BF),
        t2=vm((512, 768), BF),
        h1t=vm((768, 768), BF),
        q=vm((512, 768), BF),
        kv=vm((4, 208, 1536), BF),
        pt=vm((4, 6, 208, 256), BF),
        cnt=vm((4, 6, 16, 256), F32),
        mask=vm((192, 256), F32),
        w=vm((512, 12), F32),
        wh=vm((512, 12), BF),
        wl=vm((512, 12), BF),
        spread=vm((12, 768), BF),
        dz=vm((512, 128), BF),
        co=vm((16, 768), F32),
        agb=vm((8, 16, 768), BF),
        ot=vm((768, 512), BF),
        m=vm((512, 768), F32),
        y=vm((512, 768), F32),
        h2t=vm((768, 512), BF),
        dyb=vm((512, 768), BF),
        dm=vm((512, 768), F32),
        g=vm((512, 1024), BF),
        gt=vm((1024, 512), BF),
        du=vm((512, 1024), BF),
        dc=vm((64, 1536), F32),
        dcb=vm((8, 16, 768), BF),
        rd=vm((8, 16, 768), BF),
        hs=vm((256, 768), BF),
        hr=vm((256, 768), BF),
        sums=vm((16, 768), F32),
        bias=vm((8, 16, 128), F32),
        bias_row=vm((1, 3072), F32),
    )
    for name, (axes, order, rows, cols) in PLAN.items():
        shapes["item_" + name] = vm((2,) * 5 + (rows, cols), BF)
        for j in range(1, 5):
            shapes["buf%d_%s" % (j, name)] = vm((2,) * (4 - j) + (rows, cols), BF)
        shapes["fin_" + name] = vm((2, 2, rows, cols), BF)
    for name in dict.fromkeys(FIRST.values()):
        shapes["buf0_" + name] = vm((2,) * 4 + PLAN[name][2:], BF)
    dma = pltpu.SemaphoreType.DMA
    shapes.update(
        fsend=dma((len(NAMES), 7)),
        frecv=dma((len(NAMES), 7)),
        load=dma((8,)),
        chunk=dma((2, 9)),
        store=dma((len(NAMES) + 2,)),
        side_s=dma((17,)),
        side_r=dma((17,)),
    )
    return shapes


def block_kernel(names, *refs):
    r = SimpleNamespace(**dict(zip(names, refs)))
    place = Place(3)
    bits = place.bits
    shard = place.seq
    last_shard = lax.axis_size(SEQ) - 1

    def local(src, dst, sem):
        return pltpu.make_async_copy(src, dst, sem)

    sources = (r.hidden, r.in_proj, r.scorer, r.selected, r.cotangent, r.out_proj)
    loads = []
    for i, (source, place_here) in enumerate(zip(sources, (r.x, r.win, r.wsc, r.sel, r.dyb, r.wout))):
        loads.append(pltpu.make_async_copy(source, place_here, r.load.at[i]))
        loads[i].start()
    x_load, win_load, wsc_load, sel_load, dyb_load, wout_load = loads

    def chunk_loads(c):
        slot = c % 2
        copies = [pltpu.make_async_copy(r.down_proj.at[:, c], r.dnc.at[slot], r.chunk.at[slot, 8])]
        for s in range(8):
            src = r.up_proj.at[:, 384 * s + 128 * c : 384 * s + 128 * c + 128]
            dst = r.upc.at[slot, :, 128 * s : 128 * s + 128]
            copies.append(pltpu.make_async_copy(src, dst, r.chunk.at[slot, s]))
        return copies

    flows = {}
    for i, name in enumerate(NAMES):
        axes, order, rows, cols = PLAN[name]
        bufs = [getattr(r, "buf0_" + FIRST[name])] + [getattr(r, "buf%d_%s" % (j, name)) for j in range(1, 5)]
        flows[name] = Flow(
            place, axes, ORDERS[order], getattr(r, "item_" + name), bufs, getattr(r, "fin_" + name), r.fsend.at[i], r.frecv.at[i]
        )

    points = iter(SCHEDULE)

    def point():
        for i in next(points):
            flows[NAMES[int(i, 16)]].advance()

    def by_column(lhs, rhs, name):
        item = flows[name].item
        out = dot(lhs, rhs).astype(BF)
        for t in range(out.shape[1] // 256):
            for k in range(2):
                half = out[:, 256 * t + 128 * k : 256 * t + 128 * k + 128]
                item[k, :, :, :, :, :, 128 * t : 128 * t + 128] = half.reshape(2, 2, 2, 2, 48, 128)
        flows[name].advance()
        point()

    r.agb[...] = jnp.zeros_like(r.agb)
    r.rd[...] = jnp.zeros_like(r.rd)
    place.greet()

    def halo(i):
        seqs = slice(2 * i, 2 * i + 2)
        return place.copy(r.hidden.at[seqs, 64:128, :], r.xh.at[seqs], r.side_s.at[16 * i], r.side_r.at[16 * i], 1)

    @pl.when(shard < last_shard)
    def _():
        halo(0).start()

    for cp in chunk_loads(0):
        cp.start()

    g1, s1, g2, s2 = (v[...].astype(F32).reshape(1, 768) for v in (r.gain_one, r.shift_one, r.gain_two, r.shift_two))
    r.bias_row[...] = r.up_bias[...].astype(F32).reshape(1, 3072)

    r.bias[...] = jnp.zeros_like(r.bias)

    x_load.wait()

    def first_norm(s, carry):
        xhat, _ = normal(r.x[s].astype(F32))
        low = (xhat * g1 + s1).astype(BF)
        r.t1[slice(s * 128, s * 128 + 128), :] = low
        r.h1t[:, slice(s * 128, s * 128 + 128)] = low.T
        return carry

    for s in range(4):
        first_norm(s, 0)
    win_load.wait()
    wsc_load.wait()

    for i in range(2):
        out = dot(r.t1[256 * i : 256 * i + 256, :], r.win[:, 768:2304]).astype(BF)
        for s in range(2):
            r.kv[2 * i + s, 64:192, :] = out[128 * s : 128 * s + 128]
    weight = jax.nn.sigmoid(dot_rt(r.t1[0:512, :], r.wsc[...]))
    high = weight.astype(BF)
    r.w[...] = weight
    r.wh[...] = high
    r.wl[...] = (weight - high.astype(F32)).astype(BF)
    head = lax.broadcasted_iota(jnp.int32, (12, 768), 0)
    column = lax.broadcasted_iota(jnp.int32, (12, 768), 1)
    r.spread[...] = ((column >= head * 64) & (column < head * 64 + 64)).astype(F32).astype(BF)

    def spread_weight(s):
        rows = slice(128 * s, 128 * s + 128)
        return dot(r.wh[rows, :], r.spread[...]) + dot(r.wl[rows, :], r.spread[...])

    for s in range(4):
        wide = spread_weight(s)
        for part in range(2):
            values = r.kv[s, 64:192, 768 * part : 768 * part + 768].astype(F32)
            pooled = (wide * values).reshape(2, 64, 768).sum(axis=1) * 0.125
            r.co[8 * part + 2 * s : 8 * part + 2 * s + 2, :] = pooled
    r.agb[shard] = r.co[...].astype(BF)

    def ahead(i):
        block = r.agb.at[shard]
        return place.copy(block, block, r.side_s.at[i], r.side_r.at[i], i)

    for i in range(1, 8):

        @pl.when(shard + i < 8)
        def _(i=i):
            ahead(i).start()

    @pl.when(shard < last_shard)
    def _():
        halo(1).start()

    r.q[...] = dot(r.t1[0:512, :], r.win[:, 0:768]).astype(BF) * jnp.asarray(0.125, BF)

    row = lax.broadcasted_iota(jnp.int32, (192, 256), 0)
    query = lax.broadcasted_iota(jnp.int32, (192, 256), 1) % 128
    inside = (row >= query) & (row <= query + 64) & ((row >= 64) | (shard > 0))
    r.mask[...] = jnp.where(inside, 0.0, NEG)
    sel_load.wait()
    own = lax.broadcasted_iota(jnp.int32, (128, 128), 0) // 64 == lax.broadcasted_iota(jnp.int32, (128, 128), 1) // 64
    own = own.astype(F32).astype(BF)
    tile_row = lax.broadcasted_iota(jnp.int32, (1, 16, 128), 1)
    before = tile_row < 2 * shard + lax.broadcasted_iota(jnp.int32, (1, 16, 128), 2) // 64
    for s in range(4):
        picks = jnp.concatenate([r.sel[s, :, 0], r.sel[s, :, 1]], axis=1)
        same = (picks[:, None, :] == tile_row).astype(F32).astype(BF)
        counts = dot(same.reshape(192, 128), own).reshape(12, 16, 128)
        counts = jnp.where(before, counts, 0.0)
        for p in range(6):
            r.cnt[s, p] = jnp.concatenate([counts[2 * p], counts[2 * p + 1]], axis=1)

    dyb_load.wait()
    in_shard = lax.broadcasted_iota(jnp.int32, (128, 768), 0) + shard * 128
    for s in range(4):
        rows = slice(128 * s, 128 * s + 128)
        keep = in_shard < r.lengths[s]
        r.dyb[rows, :] = jnp.where(keep, r.dyb[rows, :].astype(F32), 0.0).astype(BF)

    chunk_loads(0)[0].wait()
    r.du[...] = dot_rt(r.dyb[...], r.dnc[0].reshape(1024, 768)).astype(BF)

    def placing(part):
        to = lax.broadcasted_iota(jnp.int32, (64, 128), 0)
        at = lax.broadcasted_iota(jnp.int32, (64, 128), 1)
        seq, tile = to // 16, to % 16
        return (at == (tile // 2) * 16 + 8 * part + 2 * seq + tile % 2).astype(F32).astype(BF)

    def tiles_from_others():
        for i in range(1, 8):

            @pl.when(shard >= i)
            def _(i=i):
                ahead(i).wait_recv()


        everything = r.agb[...].reshape(128, 768)
        for part in range(2):
            placed = dot(placing(part), everything).astype(BF)
            for s in range(4):
                r.kv[s, 192:208, 768 * part : 768 * part + 768] = placed[16 * s : 16 * s + 16]

    def pair_block(ref, p):
        return ref.at[208 * (p // 3) : 208 * (p // 3) + 208, 256 * (p % 3) : 256 * (p % 3) + 256]

    def halo_tiles(i):
        @pl.when(shard == 0)
        def _():
            r.xh[2 * i : 2 * i + 2] = jnp.zeros((2, 64, 768), BF)

        @pl.when(shard > 0)
        def _():
            halo(i).wait_recv()

        rows = slice(512 + 128 * i, 640 + 128 * i)
        xhat, _ = normal(r.xh[2 * i : 2 * i + 2].reshape(128, 768).astype(F32))
        low = (xhat * g1 + s1).astype(BF)
        r.h1t[:, rows] = low.T
        out = dot(low, r.win[:, 768:2304]).astype(BF)
        for s in range(2):
            r.kv[2 * i + s, 0:64, :] = out[64 * s : 64 * s + 64]

    def attend(s):
        rows = slice(s * 128, s * 128 + 128)
        for p in range(6):
            col = slice(128 * p, 128 * p + 128)
            pair_block(r.y, p)[...] = dot_rt(r.kv[s, :, col], heads_apart(r.q[rows, col]))
        for p in range(6):
            for h in range(2):
                lane = slice(128 * h, 128 * h + 128)
                scores = pair_block(r.y, p)
                count = r.cnt[s, p, :, lane]
                near = scores[:192, lane] + r.mask[:, lane]
                far = jnp.where(count > 0, scores[192:, lane], NEG)
                top = jnp.maximum(jnp.max(near, axis=0, keepdims=True), jnp.max(far, axis=0, keepdims=True))
                near = jnp.exp(near - top)
                far = count * jnp.exp(far - top)
                total = jnp.sum(near, axis=0, keepdims=True) + jnp.sum(far, axis=0, keepdims=True)
                scale = 1.0 / total
                r.pt[s, p, 0:192, lane] = (near * scale).astype(BF)
                r.pt[s, p, 192:208, lane] = (far * scale).astype(BF)
        for p in range(6):
            col = slice(128 * p, 128 * p + 128)
            values = r.kv[s, :, 768 + 128 * p : 896 + 128 * p]
            r.ot[col, rows] = heads_joined(dot_lt(values, r.pt[s, p])).astype(BF)
        r.t2[rows, :] = r.ot[:, rows].T

    def second_norm(s):
        rows = slice(s * 128, s * 128 + 128)
        xhat, _ = normal(r.m[rows, :])
        low = (xhat * g2 + s2).astype(BF)
        r.t1[rows, :] = low
        r.h2t[:, rows] = low.T

    def units(c, i):
        up, down = r.upc.at[c % 2], r.dnc.at[c % 2]
        bias = jnp.concatenate([r.bias_row[:, 384 * j + 128 * c : 384 * j + 128 * c + 128] for j in range(8)], axis=1)
        root = math.sqrt(2.0 / math.pi)
        rows = slice(256 * i, 256 * i + 256)
        u = dot(r.t1[rows, :], up[...]) + bias
        dg = dot_rt(r.dyb[rows, :], down[...].reshape(1024, 768)) if c else r.du[rows, :].astype(F32)
        squared = u * u
        half = 0.5 + 0.5 * jnp.tanh(u * (root + root * 0.044715 * squared))
        act = u * half
        slope = half + act * (1.0 - half) * (2.0 * root + 6.0 * root * 0.044715 * squared)
        act_low = act.astype(BF)
        du = (dg * slope).astype(BF)
        r.g[rows, :] = act_low
        r.du[rows, :] = du
        r.gt[:, rows] = act_low.T
        sums = jnp.sum(du.astype(F32), axis=0, keepdims=True)
        for j in range(8):
            r.bias[j, c : c + 1, :] += sums[:, 128 * j : 128 * j + 128]

    for i in range(2):
        rows = slice(256 * i, 256 * i + 256)
        halo_tiles(i)
        if i == 0:
            tiles_from_others()
        attend(2 * i)
        attend(2 * i + 1)
        if i == 0:
            wout_load.wait()
        r.m[rows, :] = r.x[2 * i : 2 * i + 2].reshape(256, 768).astype(F32) + dot(r.t2[rows, :], r.wout[...])
        second_norm(2 * i)
        second_norm(2 * i + 1)
        if i == 0:
            for cp in chunk_loads(0)[1:]:
                cp.wait()
        units(0, i)

    for c in range(3):
        if c:
            for cp in chunk_loads(c):
                cp.wait()
        if c < 2:
            for cp in chunk_loads(c + 1):
                cp.start()
        up, down = r.upc.at[c % 2], r.dnc.at[c % 2]
        if c:
            units(c, 0)
            units(c, 1)
        point()

        def gradients(c=c):
            d_name = "d%d" % c
            item = flows[d_name].item
            item[...] = dot(r.gt[...], r.dyb[...]).astype(BF).reshape(2, 2, 2, 2, 2, 32, 768)
            flows[d_name].advance()
            point()
            by_column(r.h2t[...], r.du[...], "u%d" % c)

        if c < 2:
            gradients()
        dh = dot_rt(r.du[...], up[...])
        r.dm[...] = r.dm[...] + dh if c else dh
        point()
        if c < 2:
            y = dot(r.g[...], down[...].reshape(1024, 768))
            r.y[...] = (r.y if c else r.m)[...] + y
            point()

    r.sums[...] = jnp.zeros((16, 768), F32)

    def second_back(s, carry):
        rows = slice(s * 128, s * 128 + 128)
        xhat, scale = normal(r.m[rows, :])
        dh = r.dm[rows, :]
        r.sums[14:15, :] += jnp.sum(dh * xhat, axis=0, keepdims=True)
        r.sums[15:16, :] += jnp.sum(dh, axis=0, keepdims=True)
        dm = r.dyb[rows, :].astype(F32) + normal_back(xhat, scale, dh * g2)
        r.dm[rows, :] = dm
        r.t1[rows, :] = dm.astype(BF)
        return carry

    for s in range(4):
        second_back(s, 0)
    point()
    by_column(r.ot[...], r.t1[0:512, :], "o")

    r.t2[...] = dot_rt(r.t1[0:512, :], r.wout[...]).astype(BF)
    point()

    dq, dk, dv = r.upc.at[0], r.upc.at[1], r.dnc.at[1]
    for s in range(4):
        rows = slice(s * 128, s * 128 + 128)
        tiles = slice(s * 16, s * 16 + 16)
        for p in range(6):
            col = slice(128 * p, 128 * p + 128)
            pair_block(r.m, p)[...] = dot_rt(r.kv[s, :, 768 + 128 * p : 896 + 128 * p], heads_apart(r.t2[rows, col]))
        for p in range(6):
            for h in range(2):
                lane = slice(128 * h, 128 * h + 128)
                probs = r.pt[s, p, :, lane].astype(F32)
                dp = pair_block(r.m, p)[:, lane]
                delta = jnp.sum(probs * dp, axis=0, keepdims=True)
                pair_block(r.t1, p)[:, lane] = (probs * (dp - delta)).astype(BF)
        for p in range(6):
            col = slice(128 * p, 128 * p + 128)
            d_values = dot(r.pt[s, p], heads_apart(r.t2[rows, col]))
            dv[s, :, col] = d_values[64:192].astype(BF)
            dv[4 + s // 2, 64 * (s % 2) : 64 * (s % 2) + 64, col] = d_values[:64].astype(BF)
            r.dc[tiles, 768 + 128 * p : 896 + 128 * p] = d_values[192:]
        for p in range(6):
            col = slice(128 * p, 128 * p + 128)
            d_keys = dot(pair_block(r.t1, p)[...], heads_apart(r.q[rows, col]))
            dk[rows, col] = d_keys[64:192].astype(BF)
            dk[512 + s * 64 : 576 + s * 64, col] = d_keys[:64].astype(BF)
            r.dc[tiles, col] = d_keys[192:]
        for p in range(6):
            col = slice(128 * p, 128 * p + 128)
            d_query = heads_joined(dot_lt(r.kv[s, :, col], pair_block(r.t1, p)[...]))
            dq[rows, col] = (d_query.T * 0.125).astype(BF)
        if s % 2:
            point()

    sent = dot_lt(placing(0), r.dc[:, 0:768].astype(BF)) + dot_lt(placing(1), r.dc[:, 768:].astype(BF))
    r.dcb[...] = sent.astype(BF).reshape(8, 16, 768)

    def behind(i, source):
        return place.copy(r.dcb.at[source], r.rd.at[i], r.side_s.at[8 + i], r.side_r.at[8 + i], -i)

    for i in range(1, 8):

        @pl.when(shard >= i)
        def _(i=i):
            behind(i, shard - i).start()

    point()

    gradients()
    by_column(r.h1t[:, 0:512], dq[0:512, 0:768], "q")
    r.y[...] += dot(r.g[...], r.dnc[0].reshape(1024, 768))
    for s in range(4):
        rows = slice(128 * s, 128 * s + 128)
        keep = in_shard < r.lengths[s]
        r.g[rows, 0:768] = jnp.where(keep, r.y[rows, :], 0.0).astype(BF)
    out_copy = pltpu.make_async_copy(r.g.at[:, 0:768], r.block_out, r.store.at[len(NAMES)])
    out_copy.start()
    for i in range(1, 8):

        @pl.when(shard + i < 8)
        def _(i=i):
            behind(i, shard).wait_recv()

    point()
    pooled = r.dcb[shard].astype(F32)
    for i in range(1, 8):
        pooled += r.rd[i].astype(F32)
    r.co[...] = pooled

    r.dz[...] = jnp.zeros_like(r.dz)
    for s in range(4):
        rows = slice(128 * s, 128 * s + 128)
        wide = spread_weight(s)
        terms = jnp.zeros((128, 768), F32)
        for part in range(2):
            pair = [r.co[8 * part + 2 * s + i : 8 * part + 2 * s + i + 1, :] for i in range(2)]
            grad = jnp.concatenate([jnp.broadcast_to(row, (64, 768)) for row in pair], axis=0) * 0.125
            terms += r.kv[s, 64:192, 768 * part : 768 * part + 768].astype(F32) * grad
            if part == 0:
                dk[rows, 0:768] = (dk[rows, 0:768].astype(F32) + wide * grad).astype(BF)
            else:
                dv[s] = (dv[s].astype(F32) + wide * grad).astype(BF)
        high = terms.astype(BF)
        low = (terms - high.astype(F32)).astype(BF)
        d_weight = dot_rt(high, r.spread[...]) + dot_rt(low, r.spread[...])
        weight = r.w[rows, :]
        r.dz[rows, 0:12] = (d_weight * weight * (1.0 - weight)).astype(BF)
    point()

    by_column(r.h1t[...], dk[:, 0:768], "k")
    by_column(r.h1t[...], dv[0:6].reshape(768, 768), "v")

    out = dot_rt(dk[512:768, 0:768], r.win[:, 768:1536])
    r.y[0:256, :] = out + dot_rt(dv[4:6].reshape(256, 768), r.win[:, 1536:2304])
    for i in range(2):
        rows = slice(128 * i, 128 * i + 128)
        xhat, scale = normal(r.xh[2 * i : 2 * i + 2].reshape(128, 768).astype(F32))
        dh = r.y[rows, :]
        r.sums[12:13, :] += jnp.sum(dh * xhat, axis=0, keepdims=True)
        r.sums[13:14, :] += jnp.sum(dh, axis=0, keepdims=True)
        r.hs[rows, :] = normal_back(xhat, scale, dh * g1).astype(BF)
    back = place.copy(r.hs, r.hr, r.side_s.at[8], r.side_r.at[8], -1)

    @pl.when(shard > 0)
    def _():
        back.start()

    point()

    out = dot_rt(dq[0:512, 0:768], r.win[:, 0:768])
    out += dot_rt(dk[0:512, 0:768], r.win[:, 768:1536])
    out += dot_rt(dv[0:4].reshape(512, 768), r.win[:, 1536:2304])
    r.m[...] = out + dot(r.dz[:, 0:12], r.wsc[...])
    point()

    @pl.when(shard == last_shard)
    def _():
        r.hr[...] = jnp.zeros_like(r.hr)

    for s in range(4):
        rows = slice(s * 128, s * 128 + 128)
        xhat, scale = normal(r.x[s].astype(F32))
        dh = r.m[rows, :]
        r.sums[12:13, :] += jnp.sum(dh * xhat, axis=0, keepdims=True)
        r.sums[13:14, :] += jnp.sum(dh, axis=0, keepdims=True)
        r.dm[rows, :] += normal_back(xhat, scale, dh * g1)
    grad_copy = pltpu.make_async_copy(r.t2, r.grad_input, r.store.at[len(NAMES) + 1])

    def input_gradient():
        @pl.when(shard < last_shard)
        def _():
            back.wait_recv()

        for s in range(4):
            rows = slice(s * 128, s * 128 + 64)
            r.t2[rows, :] = r.dm[rows, :].astype(BF)
            rows = slice(s * 128 + 64, s * 128 + 128)
            r.t2[rows, :] = (r.dm[rows, :] + r.hr[s * 64 : s * 64 + 64, :].astype(F32)).astype(BF)
        grad_copy.start()

    point()

    item = flows["m"].item
    small = dot(r.h1t[:, 0:512], r.dz[...]).T[0:16] + r.sums[...]
    item[...] = jnp.zeros_like(item)
    for s in range(8):
        item[0, s // 4, (s // 2) % 2, s % 2, 0, :, 0:96] = small[:, 96 * s : 96 * s + 96].astype(BF)
        item[1, s // 4, (s // 2) % 2, s % 2, 0] = r.bias[s].astype(BF)
    flows["m"].advance()
    point()

    stores = [pltpu.make_async_copy(getattr(r, "fin_" + name), getattr(r, "out_" + name), r.store.at[i]) for i, name in enumerate(NAMES)]
    stored = set()

    def store():
        for i, name in enumerate(NAMES):
            if flows[name].done == 8 and i not in stored:
                stored.add(i)
                stores[i].start()

    store()
    for i in next(points):
        if i == "f":
            input_gradient()
        else:
            flows[NAMES[int(i, 16)]].advance()
            store()
    for i, name in enumerate(NAMES):
        flows[name].finish()
        store()
    for cp in stores:
        cp.wait()
    out_copy.wait()
    grad_copy.wait()

    @pl.when(shard < last_shard)
    def _():
        halo(0).wait_send()
        halo(1).wait_send()

    @pl.when(shard > 0)
    def _():
        back.wait_send()

    for i in range(1, 8):

        @pl.when(shard + i < 8)
        def _(i=i):
            ahead(i).wait_send()

        @pl.when(shard >= i)
        def _(i=i):
            behind(i, shard - i).wait_send()


def finish_kernel(names, *refs):
    r = SimpleNamespace(**dict(zip(names, refs)))
    copies = []
    rows_in = (pltpu.make_async_copy(r.block, r.rows.at[0], r.sems.at[0]), pltpu.make_async_copy(r.grad, r.rows.at[1], r.sems.at[1]))
    loads = {}
    for i, name in enumerate(NAMES):
        loads[name] = pltpu.make_async_copy(getattr(r, "sum_" + name), getattr(r, "fin_" + name), r.sems.at[2 + i])
    for cp in rows_in + tuple(loads.values()):
        cp.start()

    def columns(name, to, place):
        rows, cols = PLAN[name][2:]
        loads[name].wait()
        fin = getattr(r, "fin_" + name)
        for k in range(2):
            for y in range(2):
                for t in range(cols // 128):
                    at = place(2 * t + k)
                    to[48 * y : 48 * y + 48, at : at + 128] = fin[k, y, :, 128 * t : 128 * t + 128].astype(F32)

    def store(src, dst):
        copies.append(pltpu.make_async_copy(src, dst, r.sems.at[2 + len(NAMES) + len(copies)]))
        copies[-1].start()

    for cp, src, dst in zip(rows_in, (r.rows.at[0], r.rows.at[1]), (r.block_out, r.grad_input)):
        cp.wait()
        store(src, dst)
    for c in range(3):
        name = "d%d" % c
        loads[name].wait()
        r.down[128 * c : 128 * c + 128, :] = getattr(r, "fin_" + name)[...].reshape(128, 768).astype(F32)
        columns("u%d" % c, r.up, lambda i, c=c: 384 * i + 128 * c)
    store(r.down, r.grad_down)
    store(r.up, r.grad_up)
    columns("o", r.out, lambda i: 128 * i)
    store(r.out, r.grad_out)
    for g, name in enumerate("qkv"):
        columns(name, r.into, lambda i, g=g: 768 * g + 128 * i)
    store(r.into, r.grad_in)
    loads["m"].wait()
    left = r.fin_m[0, 0].astype(F32)[:, 0:96]
    r.score[...] = left[0:12]
    for i, gain in enumerate((r.grad_gain_one, r.grad_shift_one, r.grad_gain_two, r.grad_shift_two)):
        gain[...] = left[12 + i : 13 + i].reshape(96)
    rows = r.fin_m[1, 0].astype(F32)
    for c in range(3):
        r.grad_bias[128 * c : 128 * c + 128] = rows[c : c + 1].reshape(128)
    for cp in copies:
        cp.wait()


def fits(hidden_in, selected, scorer, up_proj):
    sizes = (hidden_in.shape, selected.shape, scorer.shape, up_proj.shape)
    wanted = ((4, 128, 768), (4, 2, 12, 64), (768, 12), (768, 3072))
    return sizes == wanted and (lax.axis_size(SEQ), lax.axis_size(BATCH)) == (8, 4)


def fused(
    hidden_in,
    lengths,
    selected,
    in_proj,
    scorer,
    out_proj,
    up_proj,
    up_bias,
    down_proj,
    first_gain,
    first_shift,
    second_gain,
    second_shift,
    cotangent,
):
    scratch = block_shapes()
    fins = tuple("out_" + name for name in NAMES)
    names = tuple(INPUTS) + ("block_out", "grad_input") + fins + tuple(scratch)
    piece_shapes = [(2, 2) + PLAN[name][2:] for name in NAMES]
    inputs = dict(
        hidden=hidden_in,
        lengths=lengths,
        selected=jnp.transpose(selected, (0, 2, 1, 3)),
        in_proj=in_proj,
        scorer=scorer.T,
        out_proj=out_proj,
        up_proj=up_proj,
        up_bias=up_bias,
        down_proj=down_proj.reshape(8, 3, 128, 768),
        gain_one=first_gain,
        shift_one=first_shift,
        gain_two=second_gain,
        shift_two=second_shift,
        cotangent=cotangent.reshape(512, 768),
    )
    block_out, grad_input, *sums = pl.pallas_call(
        partial(block_kernel, names),
        out_shape=[jax.ShapeDtypeStruct(shape, BF) for shape in [(512, 768)] * 2 + piece_shapes],
        in_specs=[INPUTS[name] for name in INPUTS],
        out_specs=[HELD] * (2 + len(NAMES)),
        scratch_shapes=list(scratch.values()),
        compiler_params=pltpu.CompilerParams(
            collective_id=0, has_side_effects=True, vmem_limit_bytes=64 * 2**20 - 65536
        ),
        name="block",
    )(*(inputs[name] for name in INPUTS))
    outs = dict(
        block_out=((512, 768), BF, HELD),
        grad_input=((512, 768), BF, HELD),
        grad_in=((96, 2304), F32, HELD),
        score=((12, 96), F32, NEAR),
        grad_out=((96, 768), F32, HELD),
        grad_up=((96, 3072), F32, HELD),
        grad_bias=((384,), F32, NEAR),
        grad_down=((384, 768), F32, HELD),
        grad_gain_one=((96,), F32, NEAR),
        grad_shift_one=((96,), F32, NEAR),
        grad_gain_two=((96,), F32, NEAR),
        grad_shift_two=((96,), F32, NEAR),
    )
    scratch = {"fin_" + name: pltpu.VMEM(shape, BF) for name, shape in zip(NAMES, piece_shapes)}
    scratch.update(
        rows=pltpu.VMEM((2, 512, 768), BF),
        into=pltpu.VMEM((96, 2304), F32),
        out=pltpu.VMEM((96, 768), F32),
        up=pltpu.VMEM((96, 3072), F32),
        down=pltpu.VMEM((384, 768), F32),
        sems=pltpu.SemaphoreType.DMA((len(NAMES) + 8,)),
    )
    names = ("block", "grad") + tuple("sum_" + name for name in NAMES) + tuple(outs) + tuple(scratch)
    block_out, grad_input, grad_in, score, *rest = pl.pallas_call(
        partial(finish_kernel, names),
        out_shape=[jax.ShapeDtypeStruct(shape, kind) for shape, kind, spec in outs.values()],
        in_specs=[HELD] * (2 + len(NAMES)),
        out_specs=[spec for shape, kind, spec in outs.values()],
        scratch_shapes=list(scratch.values()),
        compiler_params=pltpu.CompilerParams(vmem_limit_bytes=64 * 2**20 - 65536),
        name="finish",
    )(block_out, grad_input, *sums)
    return (block_out.reshape(4, 128, 768), grad_input.reshape(4, 128, 768), grad_in, score.T, *rest)


def shards(
    hidden_in,
    lengths,
    selected,
    in_proj,
    scorer,
    out_proj,
    up_proj,
    up_bias,
    down_proj,
    first_gain,
    first_shift,
    second_gain,
    second_shift,
    cotangent,
):
    if fits(hidden_in, selected, scorer, up_proj):
        return fused(
            hidden_in,
            lengths,
            selected,
            in_proj,
            scorer,
            out_proj,
            up_proj,
            up_bias,
            down_proj,
            first_gain,
            first_shift,
            second_gain,
            second_shift,
            cotangent,
        )
    sequences, tokens, model_width = hidden_in.shape
    head_count = scorer.shape[1]
    head_size = model_width // head_count
    tile_count = tokens // TILE
    row_count = sequences * tokens
    span = 2 * TILE
    score_scale = 1.0 / math.sqrt(head_size)
    root_tile = math.sqrt(TILE)
    gain_one = first_gain.astype(jnp.float32)
    shift_one = first_shift.astype(jnp.float32)
    gain_two = second_gain.astype(jnp.float32)
    shift_two = second_shift.astype(jnp.float32)
    hidden = hidden_in.astype(jnp.float32).reshape(row_count, model_width)
    normed = layer_norm(hidden, gain_one, shift_one).astype(jnp.bfloat16)
    packed = jnp.dot(normed, in_proj, preferred_element_type=jnp.float32).astype(jnp.bfloat16)
    weights = jax.nn.sigmoid(jnp.dot(normed, scorer, preferred_element_type=jnp.float32))
    shaped = packed.reshape(sequences, tile_count, TILE, 3, head_count, head_size)
    query_tiles = shaped[:, :, :, 0]
    pair_tiles = shaped[:, :, :, 1:]
    key_float = pair_tiles[:, :, :, 0].astype(jnp.float32)
    value_float = pair_tiles[:, :, :, 1].astype(jnp.float32)
    tile_weights = weights.reshape(sequences, tile_count, TILE, head_count, 1)
    key_comp = jnp.sum(tile_weights * key_float, axis=2) / root_tile
    value_comp = jnp.sum(tile_weights * value_float, axis=2) / root_tile
    compressed = jnp.concatenate(
        [
            key_comp.reshape(sequences, tile_count, model_width),
            value_comp.reshape(sequences, tile_count, model_width),
        ],
        -1,
    ).astype(jnp.bfloat16)
    gathered = lax.all_gather(compressed, SEQ, axis=1, tiled=True)
    last_rows = packed.reshape(sequences, tokens, 3 * model_width)[:, tokens - TILE :, model_width:]
    previous = passed_along(last_rows, SEQ, 1)
    previous = previous.reshape(sequences, 1, TILE, 2, head_count, head_size)
    before = jnp.concatenate([previous, pair_tiles[:, :-1]], 1)
    window_pairs = jnp.concatenate([before, pair_tiles], 2)
    key_window = window_pairs[:, :, :, 0]
    value_window = window_pairs[:, :, :, 1]
    tile_total = gathered.shape[1]
    choose = (selected[..., None] == jnp.arange(tile_total, dtype=jnp.int32)).astype(jnp.bfloat16)
    gathered_split = gathered.reshape(sequences, tile_total, 2, head_count, head_size)
    key_pick = jnp.einsum(
        "sphjn,snhd->sphjd", choose, gathered_split[:, :, 0], preferred_element_type=jnp.float32
    ).astype(jnp.bfloat16)
    value_pick = jnp.einsum(
        "sphjn,snhd->sphjd", choose, gathered_split[:, :, 1], preferred_element_type=jnp.float32
    ).astype(jnp.bfloat16)
    tile_ids = lax.axis_index(SEQ) * tile_count + jnp.arange(tile_count, dtype=jnp.int32)
    allowed = allowed_mask(tile_ids, selected)
    scores = attention_scores(query_tiles, key_window, key_pick, allowed, score_scale)
    top_score = jnp.max(scores, -1, keepdims=True)
    log_total = top_score + jnp.log(jnp.sum(jnp.exp(scores - top_score), -1, keepdims=True))
    probs_low = jnp.exp(scores - log_total).astype(jnp.bfloat16)
    near_out = jnp.einsum(
        "sphab,spbhd->spahd",
        probs_low[..., :span],
        value_window,
        preferred_element_type=jnp.float32,
    )
    far_out = jnp.einsum(
        "sphaj,sphjd->spahd", probs_low[..., span:], value_pick, preferred_element_type=jnp.float32
    )
    attended = (near_out + far_out).reshape(row_count, model_width).astype(jnp.bfloat16)
    middle = hidden + jnp.dot(attended, out_proj, preferred_element_type=jnp.float32)
    normed_two = layer_norm(middle, gain_two, shift_two).astype(jnp.bfloat16)
    upper = jnp.dot(normed_two, up_proj, preferred_element_type=jnp.float32) + up_bias.astype(
        jnp.float32
    )
    gelu_fn = partial(jax.nn.gelu, approximate=True)
    active, gelu_pull = jax.vjp(gelu_fn, upper)
    active = active.astype(jnp.bfloat16)
    result = middle + jnp.dot(active, down_proj, preferred_element_type=jnp.float32)
    positions = lax.axis_index(SEQ) * tokens + jnp.arange(tokens, dtype=jnp.int32)
    valid = (positions[None, :] < lengths[:, None]).reshape(row_count, 1)
    block_out = (
        jnp.where(valid, result, 0.0).astype(jnp.bfloat16).reshape(sequences, tokens, model_width)
    )
    d_result = jnp.where(valid, cotangent.astype(jnp.float32).reshape(row_count, model_width), 0.0)
    d_result_low = d_result.astype(jnp.bfloat16)
    grad_down = jnp.einsum("rf,rd->fd", active, d_result_low, preferred_element_type=jnp.float32)
    d_active = jnp.einsum("rd,fd->rf", d_result_low, down_proj, preferred_element_type=jnp.float32)
    d_upper = gelu_pull(d_active)[0].astype(jnp.bfloat16)
    grad_up = jnp.einsum("rd,rf->df", normed_two, d_upper, preferred_element_type=jnp.float32)
    grad_up_bias = jnp.sum(d_upper.astype(jnp.float32), axis=0)
    d_normed_two = jnp.einsum("rf,df->rd", d_upper, up_proj, preferred_element_type=jnp.float32)
    ignored, norm_two_pull = jax.vjp(layer_norm, middle, gain_two, shift_two)
    d_middle_norm, grad_gain_two, grad_shift_two = norm_two_pull(d_normed_two)
    d_middle = d_result + d_middle_norm
    d_middle_low = d_middle.astype(jnp.bfloat16)
    grad_out = jnp.einsum("rd,re->de", attended, d_middle_low, preferred_element_type=jnp.float32)
    d_attended = jnp.einsum("re,de->rd", d_middle_low, out_proj, preferred_element_type=jnp.float32)
    d_attended = d_attended.astype(jnp.bfloat16).reshape(
        sequences, tile_count, TILE, head_count, head_size
    )
    scores_again = attention_scores(query_tiles, key_window, key_pick, allowed, score_scale)
    probs = jnp.exp(scores_again - log_total)
    probs_again = probs.astype(jnp.bfloat16)
    d_probs_near = jnp.einsum(
        "spahd,spbhd->sphab", d_attended, value_window, preferred_element_type=jnp.float32
    )
    d_probs_far = jnp.einsum(
        "spahd,sphjd->sphaj", d_attended, value_pick, preferred_element_type=jnp.float32
    )
    d_probs = jnp.concatenate([d_probs_near, d_probs_far], -1)
    row_delta = jnp.sum(probs * d_probs, -1, keepdims=True)
    d_scores = (probs * (d_probs - row_delta)).astype(jnp.bfloat16)
    d_near = d_scores[..., :span]
    d_far = d_scores[..., span:]
    d_query = (
        jnp.einsum("sphab,spbhd->spahd", d_near, key_window, preferred_element_type=jnp.float32)
        + jnp.einsum("sphaj,sphjd->spahd", d_far, key_pick, preferred_element_type=jnp.float32)
    ) * score_scale
    d_key_window = (
        jnp.einsum("sphab,spahd->spbhd", d_near, query_tiles, preferred_element_type=jnp.float32)
        * score_scale
    )
    d_value_window = jnp.einsum(
        "sphab,spahd->spbhd",
        probs_again[..., :span],
        d_attended,
        preferred_element_type=jnp.float32,
    )
    d_key_pick = (
        jnp.einsum("sphaj,spahd->sphjd", d_far, query_tiles, preferred_element_type=jnp.float32)
        * score_scale
    )
    d_value_pick = jnp.einsum(
        "sphaj,spahd->sphjd",
        probs_again[..., span:],
        d_attended,
        preferred_element_type=jnp.float32,
    )
    choose_float = choose.astype(jnp.float32)
    d_key_comp = jnp.einsum(
        "sphjn,sphjd->snhd", choose_float, d_key_pick, precision=lax.Precision.HIGHEST
    )
    d_value_comp = jnp.einsum(
        "sphjn,sphjd->snhd", choose_float, d_value_pick, precision=lax.Precision.HIGHEST
    )
    d_compressed = jnp.concatenate(
        [
            d_key_comp.reshape(sequences, tile_total, model_width),
            d_value_comp.reshape(sequences, tile_total, model_width),
        ],
        -1,
    )
    own_comp = sum_at_owner(d_compressed.astype(jnp.bfloat16), SEQ, 1)
    own_key_comp = own_comp[..., :model_width].reshape(
        sequences, tile_count, 1, head_count, head_size
    )
    own_value_comp = own_comp[..., model_width:].reshape(
        sequences, tile_count, 1, head_count, head_size
    )
    window_grads = jnp.stack([d_key_window, d_value_window], axis=3)
    back_part = window_grads[:, :, :TILE]
    own_part = window_grads[:, :, TILE:]
    outgoing = back_part[:, 0].reshape(sequences, TILE, 2 * model_width)
    incoming = passed_along(outgoing.astype(jnp.bfloat16), SEQ, -1).astype(outgoing.dtype)
    incoming = incoming.reshape(sequences, 1, TILE, 2, head_count, head_size)
    own_total = own_part + jnp.concatenate([back_part[:, 1:], incoming], 1)
    d_key = own_total[:, :, :, 0] + tile_weights * own_key_comp / root_tile
    d_value = own_total[:, :, :, 1] + tile_weights * own_value_comp / root_tile
    d_weights = (
        jnp.sum(key_float * own_key_comp, -1) + jnp.sum(value_float * own_value_comp, -1)
    ) / root_tile
    flat_weights = weights.reshape(sequences, tile_count, TILE, head_count)
    d_logits = (
        (d_weights * flat_weights * (1.0 - flat_weights))
        .reshape(row_count, head_count)
        .astype(jnp.bfloat16)
    )
    d_packed = (
        jnp.stack([d_query, d_key, d_value], axis=3)
        .reshape(row_count, 3 * model_width)
        .astype(jnp.bfloat16)
    )
    grad_in = jnp.einsum("rd,re->de", normed, d_packed, preferred_element_type=jnp.float32)
    grad_score = jnp.einsum("rd,rh->dh", normed, d_logits, preferred_element_type=jnp.float32)
    d_normed = jnp.einsum(
        "re,de->rd", d_packed, in_proj, preferred_element_type=jnp.float32
    ) + jnp.einsum("rh,dh->rd", d_logits, scorer, preferred_element_type=jnp.float32)
    ignored_one, norm_one_pull = jax.vjp(layer_norm, hidden, gain_one, shift_one)
    d_hidden_norm, grad_gain_one, grad_shift_one = norm_one_pull(d_normed)
    grad_input = (
        (d_middle + d_hidden_norm).astype(jnp.bfloat16).reshape(sequences, tokens, model_width)
    )
    all_shares = (
        lax.psum_scatter(grad_in, SEQ, scatter_dimension=0, tiled=True),
        lax.psum_scatter(grad_score, SEQ, scatter_dimension=0, tiled=True),
        lax.psum_scatter(grad_out, SEQ, scatter_dimension=0, tiled=True),
        lax.psum_scatter(grad_up, SEQ, scatter_dimension=0, tiled=True),
        lax.psum_scatter(grad_up_bias, SEQ, scatter_dimension=0, tiled=True),
        lax.psum_scatter(grad_down, SEQ, scatter_dimension=0, tiled=True),
        lax.psum_scatter(grad_gain_one, SEQ, scatter_dimension=0, tiled=True),
        lax.psum_scatter(grad_shift_one, SEQ, scatter_dimension=0, tiled=True),
        lax.psum_scatter(grad_gain_two, SEQ, scatter_dimension=0, tiled=True),
        lax.psum_scatter(grad_shift_two, SEQ, scatter_dimension=0, tiled=True),
    )
    ordered = (
        lax.psum(all_shares[0].astype(jnp.bfloat16), BATCH).astype(jnp.float32),
        lax.psum(all_shares[1].astype(jnp.bfloat16), BATCH).astype(jnp.float32),
        lax.psum(all_shares[2].astype(jnp.bfloat16), BATCH).astype(jnp.float32),
        lax.psum(all_shares[3].astype(jnp.bfloat16), BATCH).astype(jnp.float32),
        lax.psum(all_shares[4].astype(jnp.bfloat16), BATCH).astype(jnp.float32),
        lax.psum(all_shares[5].astype(jnp.bfloat16), BATCH).astype(jnp.float32),
        lax.psum(all_shares[6].astype(jnp.bfloat16), BATCH).astype(jnp.float32),
        lax.psum(all_shares[7].astype(jnp.bfloat16), BATCH).astype(jnp.float32),
        lax.psum(all_shares[8].astype(jnp.bfloat16), BATCH).astype(jnp.float32),
        lax.psum(all_shares[9].astype(jnp.bfloat16), BATCH).astype(jnp.float32),
    )
    return (
        block_out,
        grad_input,
        ordered[0],
        ordered[1],
        ordered[2],
        ordered[3],
        ordered[4],
        ordered[5],
        ordered[6],
        ordered[7],
        ordered[8],
        ordered[9],
    )


def solution(mesh):
    placed = (
        P(BATCH, SEQ, None),
        P(BATCH),
        P(BATCH, SEQ, None, None),
        P(),
        P(),
        P(),
        P(),
        P(),
        P(),
        P(),
        P(),
        P(),
        P(),
        P(BATCH, SEQ, None),
    )
    return jax.shard_map(
        shards,
        mesh=mesh,
        in_specs=placed,
        out_specs=(
            P(BATCH, SEQ, None),
            P(BATCH, SEQ, None),
            P(SEQ, None),
            P(SEQ, None),
            P(SEQ, None),
            P(SEQ, None),
            P(SEQ),
            P(SEQ, None),
            P(SEQ),
            P(SEQ),
            P(SEQ),
            P(SEQ),
        ),
        check_vma=False,
    )
```
